32 devices in a mesh: dp: 4 (over x, core), ctx: 2 (over y), tensor: 4 (over z).
Axes of the slice: x: 2, y: 2, z: 4, core: 2. Of those that a mesh axis runs over, the one named last changes fastest.
Arguments:
- tokens: bfloat16 [16, 1024, 1024], P('dp', ('ctx', 'tensor')), may hold values from -6 to 6
- seg_starts: int32 [16, 7], P('dp'), may hold values from 0 to 1024, as said below
- norm_gain: float32 [1024], replicated, may hold values from 0.5 to 1.5
- w_query: bfloat16 [1024, 1024], P(('dp', 'ctx'), 'tensor'), may hold values from -0.1875 to 0.1875
- w_key: bfloat16 [1024, 1024], P(('dp', 'ctx'), 'tensor'), may hold values from -0.1875 to 0.1875
- w_value: bfloat16 [1024, 2048], P(('dp', 'ctx'), 'tensor'), may hold values from -0.1875 to 0.1875
- w_gate: bfloat16 [1024, 2048], P(('dp', 'ctx'), 'tensor'), may hold values from -0.1875 to 0.1875
- w_alpha: bfloat16 [1024, 8], P(('dp', 'ctx'), 'tensor'), may hold values from -0.1875 to 0.1875
- w_beta: bfloat16 [1024, 8], P(('dp', 'ctx'), 'tensor'), may hold values from -0.1875 to 0.1875
- conv_query: float32 [4, 1024], replicated, may hold values from -3 to 3
- conv_key: float32 [4, 1024], replicated, may hold values from -3 to 3
- conv_value: float32 [4, 2048], replicated, may hold values from -3 to 3
- a_log: float32 [8], replicated, may hold values from -9 to -2.5
- dt_bias: float32 [8], replicated, may hold values from -1 to 1
- out_gain: float32 [256], replicated, may hold values from 0.5 to 1.5
- w_out: bfloat16 [2048, 1024], P('tensor', ('dp', 'ctx')), may hold values from -0.125 to 0.125
- ffn_gain: float32 [1024], replicated, may hold values from 0.5 to 1.5
- w_ffn_gate: bfloat16 [1024, 2816], P(('dp', 'ctx'), 'tensor'), may hold values from -0.1875 to 0.1875
- w_ffn_up: bfloat16 [1024, 2816], P(('dp', 'ctx'), 'tensor'), may hold values from -0.1875 to 0.1875
- w_ffn_down: bfloat16 [2816, 1024], P('tensor', ('dp', 'ctx')), may hold values from -0.109375 to 0.109375
- d_mixed: bfloat16 [16, 1024, 1024], P('dp', ('ctx', 'tensor')), may hold values from -6 to 6
Outputs:
- mixed: bfloat16 [16, 1024, 1024], P('dp', ('ctx', 'tensor'))
- grad_tokens: float32 [16, 1024, 1024], P('dp', ('ctx', 'tensor'))
- grad_norm_gain: float32 [1024], replicated
- grad_w_query: float32 [1024, 1024], P(('dp', 'ctx'), 'tensor')
- grad_w_key: float32 [1024, 1024], P(('dp', 'ctx'), 'tensor')
- grad_w_value: float32 [1024, 2048], P(('dp', 'ctx'), 'tensor')
- grad_w_gate: float32 [1024, 2048], P(('dp', 'ctx'), 'tensor')
- grad_w_alpha: float32 [1024, 8], P(('dp', 'ctx'), 'tensor')
- grad_w_beta: float32 [1024, 8], P(('dp', 'ctx'), 'tensor')
- grad_conv_query: float32 [4, 1024], replicated
- grad_conv_key: float32 [4, 1024], replicated
- grad_conv_value: float32 [4, 2048], replicated
- grad_a_log: float32 [8], replicated
- grad_dt_bias: float32 [8], replicated
- grad_out_gain: float32 [256], replicated
- grad_w_out: float32 [2048, 1024], P('tensor', ('dp', 'ctx'))
- grad_ffn_gain: float32 [1024], replicated
- grad_w_ffn_gate: float32 [1024, 2816], P(('dp', 'ctx'), 'tensor')
- grad_w_ffn_up: float32 [1024, 2816], P(('dp', 'ctx'), 'tensor')
- grad_w_ffn_down: float32 [2816, 1024], P('tensor', ('dp', 'ctx'))
The draws below stay inside these ranges and needn't reach their ends.
Inputs may be any that keep to these rules, and one draw needn't show every extreme that they name: `seg_starts`: each row lists the start positions of the documents packed into one sequence, increasing, the first 0; entries after the last document's start equal 1024, and every row has some. In each aligned group of 4 rows (the sequences of one index of dp) one row, drawn from the seed, holds three documents: a first one of at least one token, a second one that starts within the row's first 512 tokens and ends within its last 512 tokens, and a last one of at least one token. In every other row each document has 200 to 2000 tokens except the last, which the sequence's end may cut.
All inputs are finite; a program needn't handle non-finite values.
Results may differ from the reference program's by a relative error of at most 0.014.
Values may be sent and summed in bfloat16 or wider, within the bound.
No kernel may reach another device: no remote copies, remote signals or barrier semaphores. Data moves between devices by JAX's collectives and lax.ppermute only.
A program may use at most 256 MiB of HBM per device.

```python
from functools import partial
import jax
import jax.numpy as jnp
from jax import lax

D = 1024
H = 8
DV = 256
FF = 2816
CONV = 4
BLK = 64
DOC_MIN = 200
DOC_MAX = 2000
BLOCK_TOK = 512
SEQ_DEV = 4
HK = 1024
HV = 2048
SEQ_LEN = 1024
SEQS = 16
SEGS = 7


def draw_seg_starts(key, part):
    key = jax.random.fold_in(key, 7)
    length_key = jax.random.fold_in(key, 11)
    pick_key = jax.random.fold_in(key, 13)
    open_key = jax.random.fold_in(key, 17)
    close_key = jax.random.fold_in(key, 19)
    lengths = jax.random.randint(length_key, (SEQS, SEGS - 1), DOC_MIN, DOC_MAX + 1).astype(jnp.int32)
    packed = jnp.concatenate([jnp.zeros((SEQS, 1), jnp.int32), jnp.cumsum(lengths, axis=1).astype(jnp.int32)], 1)
    packed = jnp.minimum(packed, SEQ_LEN).astype(jnp.int32)
    chosen = jax.random.randint(pick_key, (SEQS // SEQ_DEV,), 0, SEQ_DEV).astype(jnp.int32)
    rows = jnp.arange(SEQS, dtype=jnp.int32)
    is_long = rows % SEQ_DEV == chosen[rows // SEQ_DEV]
    opening = jax.random.randint(open_key, (SEQS, 1), 1, BLOCK_TOK).astype(jnp.int32)
    closing = jax.random.randint(close_key, (SEQS, 1), SEQ_LEN - BLOCK_TOK + 1, SEQ_LEN).astype(jnp.int32)
    slots = jnp.arange(SEGS, dtype=jnp.int32)[None, :]
    filler = jnp.full((SEQS, SEGS), SEQ_LEN, jnp.int32)
    spanning = jnp.where(slots == 0, 0, jnp.where(slots == 1, opening, jnp.where(slots == 2, closing, filler)))
    return jnp.where(is_long[:, None], spanning, packed).astype(jnp.int32)


def level_of(rng, shape, split, smallest, high):
    loudness = 1.0
    for dim, shards_of in split:
        steps = jax.random.uniform(jax.random.fold_in(jax.random.fold_in(rng, 6), dim), (shards_of,), jnp.float32, smallest / len(split), high / len(split))
        loudness = loudness * jnp.repeat(jnp.exp(steps), shape[dim] // shards_of).reshape((-1,) + (1,) * (len(shape) - 1 - dim))
    return loudness


def centred(own_key, extent, deviation, reach, cuts=(), kind=jnp.bfloat16):
    factor_of = level_of(own_key, extent, cuts, -0.22, 0.18) if cuts else 1.0
    values = jax.random.normal(own_key, extent, jnp.float32) * deviation * factor_of
    return jnp.minimum(jnp.maximum(values, -reach), reach).astype(kind)


def setup_inputs(seed: int = 0) -> dict:
    keys = jax.random.split(jax.random.key(seed), 22)
    tokens = centred(keys[0], (SEQS, SEQ_LEN, D), 1.0, 6.0, ((0, 4), (1, 8)))
    seg_starts = draw_seg_starts(jax.random.fold_in(keys[21], 71), 0)
    norm_gain = jnp.clip(1.0 + 0.1 * jax.random.normal(keys[2], (D,), jnp.float32), 0.5, 1.5)
    w_query = centred(keys[3], (D, HK), D ** -0.5, 0.1875, ((0, 8), (1, 4)))
    w_key = centred(keys[4], (D, HK), D ** -0.5, 0.1875, ((0, 8), (1, 4)))
    w_value = centred(keys[5], (D, HV), D ** -0.5, 0.1875, ((0, 8), (1, 4)))
    w_gate = centred(keys[6], (D, HV), D ** -0.5, 0.1875, ((0, 8), (1, 4)))
    w_alpha = centred(keys[7], (D, H), D ** -0.5, 0.1875, ((0, 8), (1, 4)))
    w_beta = centred(keys[8], (D, H), D ** -0.5, 0.1875, ((0, 8), (1, 4)))
    conv_query = centred(keys[9], (CONV, HK), CONV ** -0.5, 3.0, (), jnp.float32)
    conv_key = centred(keys[10], (CONV, HK), CONV ** -0.5, 3.0, (), jnp.float32)
    conv_value = centred(keys[11], (CONV, HV), CONV ** -0.5, 3.0, (), jnp.float32)
    a_log = jnp.clip(jax.random.uniform(keys[12], (H,), jnp.float32, -9.0, -2.5), -9.0, -2.5)
    dt_bias = jnp.clip(jax.random.uniform(keys[13], (H,), jnp.float32, -1.0, 1.0), -1.0, 1.0)
    out_gain = jnp.clip(1.0 + 0.1 * jax.random.normal(keys[14], (DV,), jnp.float32), 0.5, 1.5)
    w_out = centred(keys[15], (HV, D), HV ** -0.5, 0.125, ((0, 4), (1, 8)))
    ffn_gain = jnp.clip(1.0 + 0.1 * jax.random.normal(keys[16], (D,), jnp.float32), 0.5, 1.5)
    w_ffn_gate = centred(keys[17], (D, FF), D ** -0.5, 0.1875, ((0, 8), (1, 4)))
    w_ffn_up = centred(keys[18], (D, FF), D ** -0.5, 0.1875, ((0, 8), (1, 4)))
    w_ffn_down = centred(keys[19], (FF, D), FF ** -0.5, 0.109375, ((0, 4), (1, 8)))
    d_mixed = centred(keys[20], (SEQS, SEQ_LEN, D), 1.0, 6.0, ((0, 4), (1, 8)))
    return dict(tokens=tokens, seg_starts=seg_starts, norm_gain=norm_gain, w_query=w_query, w_key=w_key, w_value=w_value, w_gate=w_gate, w_alpha=w_alpha, w_beta=w_beta, conv_query=conv_query, conv_key=conv_key, conv_value=conv_value, a_log=a_log, dt_bias=dt_bias, out_gain=out_gain, w_out=w_out, ffn_gain=ffn_gain, w_ffn_gate=w_ffn_gate, w_ffn_up=w_ffn_up, w_ffn_down=w_ffn_down, d_mixed=d_mixed)


EPS_NORM = 1e-05
EPS_UNIT = 1e-06
FULL_ACCURACY = lax.Precision.HIGHEST

@jax.custom_vjp
def low(v):
    return lax.optimization_barrier(v.astype(jnp.bfloat16)).astype(jnp.float32)

@jax.custom_vjp
def low_back(v):
    return v

def low_keep(v):
    return (low(v), None)

def low_pass(kept, grad):
    return (grad,)

def back_keep(v):
    return (v, None)

def back_low(kept, grad):
    return (low(grad),)
low.defvjp(low_keep, low_pass)
low_back.defvjp(back_keep, back_low)

def seg_ids(starts, positions):
    return lax.optimization_barrier(jnp.sum((starts[None, :] <= positions[:, None]).astype(jnp.int32), axis=1)) - 1

def rms_rows(values):
    return values * lax.rsqrt(lax.optimization_barrier(jnp.mean(values * values, axis=-1, keepdims=True)) + EPS_NORM)

def unit_rows(values):
    return values * lax.rsqrt(lax.optimization_barrier(jnp.sum(values * values, axis=-1, keepdims=True)) + EPS_UNIT)

def product(left, right):
    return jnp.dot(left.astype(jnp.float32), right.astype(jnp.float32), precision=FULL_ACCURACY, preferred_element_type=jnp.float32)

def short_conv(extended, taps, seg_ext):
    count = taps.shape[0]
    length = extended.shape[0] - (count - 1)
    target = seg_ext[count - 1:]
    total = jnp.zeros((length, extended.shape[1]), extended.dtype)
    for offset in range(count):
        first = count - 1 - offset
        shifted = extended[first:first + length]
        inside = (seg_ext[first:first + length] == target).astype(extended.dtype)
        total = total + taps[offset] * shifted * inside[:, None]
    return total

def prepare(ext_query, ext_key, ext_value, pre_alpha, pre_beta, taps_query, taps_key, taps_value, log_scale, decay_bias, seg_ext):
    length, heads = pre_alpha.shape
    query_rows = jax.nn.silu(short_conv(ext_query, taps_query, seg_ext)).reshape(length, heads, -1)
    key_rows = jax.nn.silu(short_conv(ext_key, taps_key, seg_ext)).reshape(length, heads, -1)
    values = jax.nn.silu(short_conv(ext_value, taps_value, seg_ext)).reshape(length, heads, -1)
    query_rows = unit_rows(query_rows) * query_rows.shape[-1] ** (-0.5)
    key_rows = unit_rows(key_rows)
    decay = jnp.transpose(-jnp.exp(log_scale) * jax.nn.softplus(pre_alpha + decay_bias))
    strength = jnp.transpose(jax.nn.sigmoid(pre_beta))
    return (jnp.transpose(query_rows, (1, 0, 2)), jnp.transpose(key_rows, (1, 0, 2)), jnp.transpose(values, (1, 0, 2)), decay, strength)

def delta_block(running_state, query_rows, key_rows, values, decay, strength, seg, seg_prev, outputs):
    width = seg.shape[0]
    cumul = jnp.cumsum(decay, axis=1)
    same_doc = seg[:, None] == seg[None, :]
    lower = jnp.tri(width, dtype=bool)
    strict = jnp.tri(width, k=-1, dtype=bool)
    allowed = (lower & same_doc)[None]
    spread = cumul[:, :, None] - cumul[:, None, :]
    within = jnp.exp(jnp.where(allowed, spread, 0.0)) * allowed
    carried = (seg == seg_prev).astype(cumul.dtype)
    opening_state = jnp.exp(cumul) * carried[None, :]
    inner = jnp.einsum('hik,hjk->hij', key_rows, key_rows, precision=FULL_ACCURACY)
    system = jnp.eye(width, dtype=cumul.dtype)[None] + strength[:, :, None] * within * inner * strict[None]
    known_state = jnp.einsum('yzd,ydf->yzf', key_rows, running_state, precision=FULL_ACCURACY)
    right_side = strength[:, :, None] * (values - opening_state[:, :, None] * known_state)
    state_update = jax.scipy.linalg.solve_triangular(system, right_side, lower=True, unit_diagonal=True)
    last_doc = seg == seg[-1]
    closing_state = jnp.exp(jnp.where(last_doc[None, :], cumul[:, -1:] - cumul, 0.0)) * last_doc[None, :].astype(cumul.dtype)
    updated_state = opening_state[:, -1][:, None, None] * running_state + jnp.einsum('nqu,nql->nul', closing_state[:, :, None] * key_rows, state_update, precision=FULL_ACCURACY)
    if outputs:
        scores = jnp.einsum('hik,hjk->hij', query_rows, key_rows, precision=FULL_ACCURACY) * within
        layer_result = opening_state[:, :, None] * jnp.einsum('yzd,ydf->yzf', query_rows, running_state, precision=FULL_ACCURACY)
        layer_result = layer_result + jnp.einsum('hij,hjv->hiv', scores, state_update, precision=FULL_ACCURACY)
        return (updated_state, layer_result)
    return (updated_state, None)

def delta_run(running_state, query_rows, key_rows, values, decay, strength, seg, seg_before, block, outputs):
    heads, length = decay.shape
    count = length // block

    def split_blocks(array):
        shaped = array.reshape((heads, count, block) + array.shape[2:])
        return jnp.moveaxis(shaped, 1, 0)
    step_block = jax.checkpoint(partial(delta_block, outputs=outputs))

    def one_block(carry_state, items):
        return step_block(carry_state, items[0], items[1], items[2], items[3], items[4], items[5], items[6])
    items = (split_blocks(query_rows), split_blocks(key_rows), split_blocks(values), split_blocks(decay), split_blocks(strength), seg.reshape(count, block), seg_before)
    final_state, pieces = lax.scan(one_block, running_state, items)
    if outputs:
        return (final_state, jnp.moveaxis(pieces, 0, 1).reshape(heads, length, -1))
    return (final_state, None)

def gate_norm(mixer_out, pre_gate, gain):
    heads, length, width = mixer_out.shape
    normed = rms_rows(mixer_out) * gain
    merged = jnp.transpose(normed, (1, 0, 2)).reshape(length, heads * width)
    return merged * jax.nn.silu(pre_gate)

def layer_sequence(inputs, starts, params):
    norm_gain, w_query, w_key, w_value, w_gate, w_alpha, w_beta, conv_query, conv_key, conv_value, a_log, dt_bias, out_gain, w_out, ffn_gain, w_ffn_gate, w_ffn_up, w_ffn_down = params
    length = inputs.shape[0]
    taps = conv_query.shape[0]
    seg_ext = seg_ids(starts, jnp.arange(-(taps - 1), length, dtype=jnp.int32))
    seg = seg_ext[taps - 1:]
    seg_before = seg_ids(starts, jnp.arange(0, length, BLK, dtype=jnp.int32) - 1)
    normed = low(rms_rows(inputs) * norm_gain)
    pre_query = low_back(product(normed, w_query))
    pre_key = low_back(product(normed, w_key))
    pre_value = low_back(product(normed, w_value))
    pre_gate = low_back(product(normed, w_gate))
    pre_alpha = low_back(product(normed, w_alpha))
    pre_beta = low_back(product(normed, w_beta))
    padding = ((taps - 1, 0), (0, 0))
    query_rows, key_rows, values, decay, strength = prepare(jnp.pad(pre_query, padding), jnp.pad(pre_key, padding), jnp.pad(pre_value, padding), pre_alpha, pre_beta, conv_query, conv_key, conv_value, a_log, dt_bias, seg_ext)
    heads = decay.shape[0]
    running_state = jnp.zeros((heads, key_rows.shape[-1], values.shape[-1]), jnp.float32)
    final_state, mixer_out = delta_run(running_state, query_rows, key_rows, values, decay, strength, seg, seg_before, BLK, True)
    gated = low(gate_norm(mixer_out, pre_gate, out_gain))
    middle = inputs + low_back(product(gated, w_out))
    normed_two = low(rms_rows(middle) * ffn_gain)
    gate_pre = low_back(product(normed_two, w_ffn_gate))
    up_pre = low_back(product(normed_two, w_ffn_up))
    hidden = low(jax.nn.silu(gate_pre) * up_pre)
    return middle + product(hidden, w_ffn_down)

def reference(tokens, seg_starts, norm_gain, w_query, w_key, w_value, w_gate, w_alpha, w_beta, conv_query, conv_key, conv_value, a_log, dt_bias, out_gain, w_out, ffn_gain, w_ffn_gate, w_ffn_up, w_ffn_down, d_mixed):
    params = tuple((item.astype(jnp.float32) for item in (norm_gain, w_query, w_key, w_value, w_gate, w_alpha, w_beta, conv_query, conv_key, conv_value, a_log, dt_bias, out_gain, w_out, ffn_gain, w_ffn_gate, w_ffn_up, w_ffn_down)))
    inputs = tokens.astype(jnp.float32)

    def forward(inputs, params):
        return lax.map(lambda pair: layer_sequence(pair[0], pair[1], params), (inputs, seg_starts))
    layer_result, pullback = jax.vjp(forward, inputs, params)
    grad_inputs, grad_params = pullback(d_mixed.astype(jnp.float32))
    g_norm, g_query, g_key, g_value, g_gate, g_alpha, g_beta, g_conv_query, g_conv_key, g_conv_value, g_log, g_bias, g_out_gain, g_out, g_ffn_gain, g_ffn_gate, g_ffn_up, g_ffn_down = grad_params
    return (layer_result.astype(jnp.bfloat16), grad_inputs, g_norm, g_query, g_key, g_value, g_gate, g_alpha, g_beta, g_conv_query, g_conv_key, g_conv_value, g_log, g_bias, g_out_gain, g_out, g_ffn_gain, g_ffn_gate, g_ffn_up, g_ffn_down)
```

```python
from functools import partial

import jax
import jax.numpy as jnp
from jax import lax
from jax.experimental import pallas as pl
from jax.experimental.pallas import tpu as pltpu
from jax.sharding import Mesh, PartitionSpec as P

CHUNK = 128
RIM = 8
EPS_NORM = 1e-05
EPS_UNIT = 1e-06
FULL_ACCURACY = lax.Precision.HIGHEST
NN = (((1,), (0,)), ((), ()))
NT = (((1,), (1,)), ((), ()))
TN = (((0,), (0,)), ((), ()))


def dot_low(left, right, dims):
    return lax.dot_general(
        left.astype(jnp.bfloat16),
        right.astype(jnp.bfloat16),
        dims,
        preferred_element_type=jnp.float32,
    )


def halves(value):
    high = value.astype(jnp.bfloat16)
    return high, (value - high.astype(jnp.float32)).astype(jnp.bfloat16)


def dot_split(left, right, dims):
    left_high, left_low = halves(left)
    right_high, right_low = halves(right)
    total = lax.dot_general(left_high, right_high, dims, preferred_element_type=jnp.float32)
    total += lax.dot_general(left_high, right_low, dims, preferred_element_type=jnp.float32)
    return total + lax.dot_general(left_low, right_high, dims, preferred_element_type=jnp.float32)


def sigmoid(value):
    return 1.0 / (1.0 + jnp.exp(-value))


def positions():
    row = lax.broadcasted_iota(jnp.int32, (CHUNK, CHUNK), 0)
    col = lax.broadcasted_iota(jnp.int32, (CHUNK, CHUNK), 1)
    return row, col


def unit_lower_inverses(lowers):
    row, col = positions()
    eye = (row == col).astype(jnp.float32)
    diag = [jnp.where(row // 8 == col // 8, low, 0.0) for low in lowers]
    result = [eye - d for d in diag]
    power = [dot_split(d, d, NN) for d in diag]
    result = [x + dot_split(x, p, NN) for x, p in zip(result, power)]
    power = [dot_split(p, p, NN) for p in power]
    result = [x + dot_split(x, p, NN) for x, p in zip(result, power)]
    size = 8
    while size < CHUNK:
        across = (row // (2 * size) == col // (2 * size)) & (row // size != col // size)
        mixed = [dot_split(jnp.where(across, low, 0.0), x, NN) for low, x in zip(lowers, result)]
        result = [x - dot_split(x, m, NN) for x, m in zip(result, mixed)]
        size *= 2
    return result


KEY = 128
VAL = 256
GATE_AT = 2 * KEY + VAL
AB_AT = GATE_AT + VAL
HEAD = AB_AT + 128
VMEM_BYTES = 48 * 2**20


def thirds(value):
    high = value.astype(jnp.bfloat16)
    rest = value - high.astype(jnp.float32)
    middle = rest.astype(jnp.bfloat16)
    return high, middle, (rest - middle.astype(jnp.float32)).astype(jnp.bfloat16)


def dot_ones(ones, value, dims):
    left = ones.astype(jnp.bfloat16)
    return sum(
        lax.dot_general(left, part, dims, preferred_element_type=jnp.float32)
        for part in thirds(value)
    )


def unit(values):
    scale = lax.rsqrt(jnp.sum(values * values, axis=-1, keepdims=True) + EPS_UNIT)
    return values * scale, scale


def last_value(column):
    return column[CHUNK - 1 : CHUNK, :]


def spread_lanes(column):
    return jnp.broadcast_to(column, (CHUNK, CHUNK))


def chunk_parts(pre, par, segs, index):
    rows = slice(index * CHUNK, (index + 1) * CHUNK)
    row, col = positions()
    tile = segs[0, index]
    columns = jnp.concatenate([tile, jnp.zeros((CHUNK - 8, CHUNK), jnp.float32)], axis=0).T
    seg = columns[:, 0:1]
    masks = [(seg == columns[:, n : n + 1]).astype(jnp.float32) for n in range(1, 4)]
    shifted = pre[0, rows, AB_AT : AB_AT + 1] + par[0, 1:2, 0:1]
    strength = sigmoid(pre[0, rows, AB_AT + 1 : AB_AT + 2])
    soft = jnp.maximum(shifted, 0.0) + jnp.log1p(jnp.exp(-jnp.abs(shifted)))
    decay = par[0, 0:1, 0:1] * soft
    lower = (row >= col).astype(jnp.float32)
    cumul = dot_ones(lower, spread_lanes(decay), NN)
    allowed = (row >= col) & (seg == tile[0:1, :])
    within = jnp.where(allowed, jnp.exp(jnp.minimum(cumul - cumul.T, 0.0)), 0.0)
    cum = cumul[:, 0:1]
    opening = jnp.where(seg == tile[1:2, 0:1], jnp.exp(cum), 0.0)
    closing = jnp.where(
        seg == tile[0:1, CHUNK - 1 :], jnp.exp(jnp.minimum(last_value(cum) - cum, 0.0)), 0.0
    )
    return dict(
        rows=rows,
        masks=masks,
        shifted=shifted,
        decay=decay,
        strength=strength,
        opening=opening,
        closing=closing,
        within=within,
    )


def fill_ext(ext, rim, pre):
    ext[0:RIM, :] = rim[0, :, :GATE_AT]
    ext[RIM:, :] = pre[0, :, :GATE_AT]


def conv_chunk(ext, taps, part):
    first = RIM + part["rows"].start
    total = taps[0:1, :] * ext[first : first + CHUNK, :]
    for offset in range(1, 4):
        shifted = ext[first - offset : first - offset + CHUNK, :]
        total = total + taps[offset : offset + 1, :] * shifted * part["masks"][offset - 1]
    return total


def split_qkv(array):
    return array[:, :KEY], array[:, KEY : 2 * KEY], array[:, 2 * KEY :]


def front_kernel(
    pre, rim, taps, par, segs,
    inverse_out, step_out, push_out, read_out, base_out, end_map, end_push,
    ext,
):
    count = pre.shape[1] // CHUNK
    fill_ext(ext, rim, pre)
    row, col = positions()
    eye = (row == col).astype(jnp.float32)
    parts = [chunk_parts(pre, par, segs, n) for n in range(count)]
    convs = [conv_chunk(ext, taps, p) for p in parts]
    acts = [split_qkv(c * sigmoid(c)) for c in convs]
    queries = [unit(a[0])[0] * (float(KEY) ** -0.5) for a in acts]
    keys = [unit(a[1])[0] for a in acts]
    inner = [dot_split(k, k, NT) for k in keys]
    lowers = [
        jnp.where(row > col, p["strength"] * p["within"] * i, 0.0) for p, i in zip(parts, inner)
    ]
    inverses = unit_lower_inverses(lowers)
    scores = [dot_low(q, k, NT) * p["within"] for q, k, p in zip(queries, keys, parts)]
    known = [
        dot_low(t, p["strength"] * a[2], NN) for t, p, a in zip(inverses, parts, acts)
    ]
    write = [
        dot_low(t, p["strength"] * p["opening"] * k, NN)
        for t, p, k in zip(inverses, parts, keys)
    ]
    closed = [p["closing"] * k for p, k in zip(parts, keys)]
    steps = [
        last_value(p["opening"]) * eye - dot_low(c, w, TN)
        for p, c, w in zip(parts, closed, write)
    ]
    pushes = [dot_low(c, u, TN) for c, u in zip(closed, known)]
    total_map, total_push = steps[0], pushes[0]
    for n in range(count):
        rows = parts[n]["rows"]
        inverse_out[0, 0, rows, :] = inverses[n]
        step_out[0, 0, rows, :] = steps[n]
        push_out[0, 0, rows, :] = pushes[n]
        read_out[0, 0, rows, :] = parts[n]["opening"] * queries[n] - dot_low(
            scores[n], write[n], NN
        )
        base_out[0, 0, rows, :] = dot_low(scores[n], known[n], NN)
        if n:
            total_push = dot_low(steps[n], total_push, NN) + pushes[n]
            total_map = dot_low(steps[n], total_map, NN)
    end_map[0, 0] = total_map
    end_push[0, 0] = total_push


def output_kernel(
    state_in, step, push, read, base, pre, gain, states_out, mixer_out, gated_out
):
    count = step.shape[2] // CHUNK
    state = state_in[0, 0]
    for n in range(count):
        rows = slice(n * CHUNK, (n + 1) * CHUNK)
        states_out[0, 0, rows, :] = state
        mixer = base[0, 0, rows, :] + dot_low(read[0, 0, rows, :], state, NN)
        mixer_out[0, 0, rows, :] = mixer
        scale = lax.rsqrt(jnp.mean(mixer * mixer, axis=-1, keepdims=True) + EPS_NORM)
        gate = pre[0, rows, GATE_AT:AB_AT]
        gated_out[0, rows, :] = (mixer * scale * gain[...] * gate * sigmoid(gate)).astype(
            jnp.bfloat16
        )
        if n < count - 1:
            state = dot_low(step[0, 0, rows, :], state, NN) + push[0, 0, rows, :]


def mixer_back(d_gated, mixer_in, pre, gain, rows):
    mixer = mixer_in[0, 0, rows, :]
    scale = lax.rsqrt(jnp.mean(mixer * mixer, axis=-1, keepdims=True) + EPS_NORM)
    normed = mixer * scale
    gate = pre[0, rows, GATE_AT:AB_AT]
    sig = sigmoid(gate)
    grad = d_gated[0, rows, :]
    through = grad * gate * sig
    d_normed = through * gain[...]
    d_mixer = scale * (d_normed - normed * jnp.mean(d_normed * normed, axis=-1, keepdims=True))
    d_gate = grad * normed * gain[...] * sig * (1.0 + gate * (1.0 - sig))
    return d_mixer, d_gate, jnp.sum(through * normed, axis=0, keepdims=True)


def pull_kernel(d_gated, mixer_in, pre, gain, step, read, pull_out, start_out):
    count = step.shape[2] // CHUNK
    carried = None
    for n in reversed(range(count)):
        rows = slice(n * CHUNK, (n + 1) * CHUNK)
        d_mixer = mixer_back(d_gated, mixer_in, pre, gain, rows)[0]
        pull = dot_low(read[0, 0, rows, :], d_mixer, TN)
        pull_out[0, 0, rows, :] = pull
        if carried is None:
            carried = pull
        else:
            carried = dot_low(step[0, 0, rows, :], carried, TN) + pull
    start_out[0, 0] = carried


def back_kernel(
    pre, rim, taps, par, segs, inverse, step, states, d_gated, mixer_in, gain, pull, d_end,
    d_all_out, d_rim_out, d_small_out,
    ext, pad,
):
    length = pre.shape[1]
    count = length // CHUNK
    fill_ext(ext, rim, pre)
    row, col = positions()
    lane = col
    last_row = lax.broadcasted_iota(jnp.int32, (CHUNK, 1), 0) == CHUNK - 1
    lower = (row >= col).astype(jnp.float32)
    d_states = [None] * count
    d_states[count - 1] = d_end[0, 0]
    for n in reversed(range(1, count)):
        block = slice(n * CHUNK, (n + 1) * CHUNK)
        d_states[n - 1] = dot_low(step[0, 0, block, :], d_states[n], TN) + pull[0, 0, block, :]
    pad[:, 0:RIM, :] = jnp.zeros((4, RIM, GATE_AT), jnp.float32)
    pad[:, RIM + length :, :] = jnp.zeros((4, RIM, GATE_AT), jnp.float32)
    d_gain = jnp.zeros((1, VAL), jnp.float32)
    d_log = jnp.zeros((1, 1), jnp.float32)
    d_bias = jnp.zeros((1, 1), jnp.float32)
    d_taps = [jnp.zeros((1, GATE_AT), jnp.float32) for _ in range(4)]
    for n in range(count):
        part = chunk_parts(pre, par, segs, n)
        block, within = part["rows"], part["within"]
        strength, opening, closing = part["strength"], part["opening"], part["closing"]
        conv = conv_chunk(ext, taps, part)
        sig = sigmoid(conv)
        act_q, act_k, value = split_qkv(conv * sig)
        unit_q, scale_q = unit(act_q)
        key, scale_k = unit(act_k)
        query = unit_q * (float(KEY) ** -0.5)
        state, d_state = states[0, 0, block, :], d_states[n]
        solve = inverse[0, 0, block, :]
        grad, d_gate, d_gain_part = mixer_back(d_gated, mixer_in, pre, gain, block)
        d_gain = d_gain + d_gain_part
        rest = value - opening * dot_low(key, state, NN)
        update = dot_low(solve, strength * rest, NN)
        scores = dot_low(query, key, NT) * within
        inner = dot_low(key, key, NT) * within
        closed = closing * key
        d_update = dot_low(scores, grad, TN) + dot_low(closed, d_state, NN)
        d_right = dot_low(solve, d_update, TN)
        d_scores = dot_low(grad, update, NT)
        d_lower = jnp.where(row > col, -dot_low(d_right, update, NT), 0.0)
        d_plain = d_scores * within
        d_inner = d_lower * strength * within
        read_back = dot_low(grad, state, NT)
        known_back = -dot_low(strength * d_right, state, NT)
        closed_back = dot_low(update, d_state, NT)
        d_query = opening * read_back + dot_low(d_plain, key, NN)
        d_key = (
            dot_low(d_plain, query, TN)
            + dot_low(d_inner, key, NN)
            + dot_low(d_inner, key, TN)
            + opening * known_back
            + closing * closed_back
        )
        lower_parts = d_lower * inner
        d_strength = jnp.sum(lower_parts, axis=1, keepdims=True) + jnp.sum(
            d_right * rest, axis=1, keepdims=True
        )
        spread = d_scores * scores + strength * lower_parts
        d_opening = jnp.sum(query * read_back + key * known_back, axis=1, keepdims=True)
        d_closing = jnp.sum(key * closed_back, axis=1, keepdims=True) * closing
        through = jnp.sum(
            jnp.sum(state * d_state, axis=1, keepdims=True), axis=0, keepdims=True
        )
        end_sum = jnp.sum(d_closing, axis=0, keepdims=True) + through * last_value(opening)
        d_cumul = (
            jnp.sum(spread, axis=1, keepdims=True)
            + d_opening * opening
            - d_closing
            + jnp.where(last_row, end_sum, 0.0)
        )
        down = spread_lanes(jnp.sum(spread, axis=0, keepdims=True)).T
        d_decay = dot_ones(lower, spread_lanes(d_cumul) - down, TN)[:, 0:1]
        d_alpha = d_decay * par[0, 0:1, 0:1] * sigmoid(part["shifted"])
        d_beta = d_strength * strength * (1.0 - strength)
        d_log = d_log + jnp.sum(d_decay * part["decay"], axis=0, keepdims=True)
        d_bias = d_bias + jnp.sum(d_alpha, axis=0, keepdims=True)
        d_all_out[0, block, GATE_AT:AB_AT] = d_gate.astype(jnp.bfloat16)
        d_all_out[0, block, AB_AT:] = jnp.where(
            lane == 0, d_alpha, jnp.where(lane == 1, d_beta, 0.0)
        ).astype(jnp.bfloat16)
        d_query = d_query * (float(KEY) ** -0.5)
        d_act = jnp.concatenate(
            [
                scale_q * (d_query - unit_q * jnp.sum(unit_q * d_query, axis=-1, keepdims=True)),
                scale_k * (d_key - key * jnp.sum(key * d_key, axis=-1, keepdims=True)),
                strength * d_right,
            ],
            axis=1,
        )
        d_conv = d_act * sig * (1.0 + conv * (1.0 - sig))
        first = RIM + block.start
        for offset in range(4):
            masked = d_conv if offset == 0 else d_conv * part["masks"][offset - 1]
            shifted = ext[first - offset : first - offset + CHUNK, :]
            d_taps[offset] = d_taps[offset] + jnp.sum(masked * shifted, axis=0, keepdims=True)
            pad[offset, first : first + CHUNK, :] = masked * taps[offset : offset + 1, :]
    d_rim = pad[0, 0:RIM, :]
    for offset in range(1, 4):
        d_rim = d_rim + pad[offset, offset : offset + RIM, :]
    d_rim_out[0] = d_rim
    for n in range(count):
        first = RIM + n * CHUNK
        total = pad[0, first : first + CHUNK, :]
        for offset in range(1, 4):
            total = total + pad[offset, first + offset : first + offset + CHUNK, :]
        d_all_out[0, n * CHUNK : (n + 1) * CHUNK, :GATE_AT] = total.astype(jnp.bfloat16)
    for offset in range(4):
        d_small_out[0, 0, offset : offset + 1, :] = d_taps[offset]
    d_small_out[0, 0, 4:5, :] = jnp.concatenate([d_gain, d_gain], axis=1)
    d_small_out[0, 0, 5:6, :] = jnp.broadcast_to(d_log, (1, GATE_AT))
    d_small_out[0, 0, 6:7, :] = jnp.broadcast_to(d_bias, (1, GATE_AT))
    d_small_out[0, 0, 7:8, :] = jnp.zeros((1, GATE_AT), jnp.float32)


def per_head(*tail):
    return pl.BlockSpec((1, 1) + tail, lambda s, h: (s, h) + (0,) * len(tail))


def lanes_at(rows, width):
    return pl.BlockSpec((1, rows, width), lambda s, h: (s, 0, h))


def front_specs(length):
    return [
        lanes_at(length, HEAD),
        lanes_at(RIM, HEAD),
        pl.BlockSpec((4, GATE_AT), lambda s, h: (0, h)),
        pl.BlockSpec((1, 8, 128), lambda s, h: (h, 0, 0)),
        pl.BlockSpec((1, length // CHUNK, 8, CHUNK), lambda s, h: (s, 0, 0, 0)),
    ]


def gain_spec():
    return pl.BlockSpec((1, VAL), lambda s, h: (0, 0))


def shape(dims, kind=jnp.float32):
    return jax.ShapeDtypeStruct(dims, kind)


def call(kernel, lead, in_specs, outs, scratch, units, args):
    length = args[0].shape[1] if args[0].ndim == 3 else args[1].shape[2]
    flops = lead[0] * lead[1] * length * 128 * 128 * 2 * units
    return pl.pallas_call(
        kernel,
        grid=lead,
        in_specs=in_specs,
        out_specs=[spec for spec, _ in outs],
        out_shape=[kind for _, kind in outs],
        scratch_shapes=[pltpu.VMEM(dims, jnp.float32) for dims in scratch],
        compiler_params=pltpu.CompilerParams(vmem_limit_bytes=VMEM_BYTES),
        cost_estimate=pl.CostEstimate(
            flops=flops, bytes_accessed=flops // 100, transcendentals=0
        ),
    )(*args)


def run_front(pre, rim, taps, par, segs):
    seqs, length, wide = pre.shape
    lead = (seqs, wide // HEAD)
    widths = (KEY, KEY, VAL, KEY, VAL)
    outs = [(per_head(length, width), shape(lead + (length, width))) for width in widths]
    outs += [(per_head(KEY, width), shape(lead + (KEY, width))) for width in (KEY, VAL)]
    return call(
        front_kernel,
        lead,
        front_specs(length),
        outs,
        [(length + RIM, GATE_AT)],
        60,
        (pre, rim, taps, par, segs),
    )


def run_output(state_in, step, push, read, base, pre, gain):
    seqs, heads, length, _ = step.shape
    lead = (seqs, heads)
    in_specs = [per_head(KEY, VAL)]
    in_specs += [per_head(length, width) for width in (KEY, VAL, KEY, VAL)]
    in_specs += [lanes_at(length, HEAD), gain_spec()]
    outs = [
        (per_head(length, VAL), shape(lead + (length, VAL))),
        (per_head(length, VAL), shape(lead + (length, VAL))),
        (lanes_at(length, VAL), shape((seqs, length, heads * VAL), jnp.bfloat16)),
    ]
    args = (state_in, step, push, read, base, pre, gain)
    return call(output_kernel, lead, in_specs, outs, [], 15, args)


def run_pull(d_gated, mixer, pre, gain, step, read):
    seqs, heads, length, _ = step.shape
    lead = (seqs, heads)
    in_specs = [lanes_at(length, VAL), per_head(length, VAL), lanes_at(length, HEAD)]
    in_specs += [gain_spec(), per_head(length, KEY), per_head(length, KEY)]
    outs = [
        (per_head(length, VAL), shape(lead + (length, VAL))),
        (per_head(KEY, VAL), shape(lead + (KEY, VAL))),
    ]
    return call(
        pull_kernel, lead, in_specs, outs, [], 15, (d_gated, mixer, pre, gain, step, read)
    )


def run_back(pre, rim, taps, par, segs, inverse, step, states, d_gated, mixer, gain, pull, d_end):
    seqs, length, wide = pre.shape
    heads = wide // HEAD
    lead = (seqs, heads)
    in_specs = front_specs(length)
    in_specs += [per_head(length, width) for width in (KEY, KEY, VAL)]
    in_specs += [lanes_at(length, VAL), per_head(length, VAL), gain_spec()]
    in_specs += [per_head(length, VAL), per_head(KEY, VAL)]
    outs = [
        (lanes_at(length, HEAD), shape((seqs, length, wide), jnp.bfloat16)),
        (lanes_at(RIM, GATE_AT), shape((seqs, RIM, heads * GATE_AT))),
        (per_head(8, GATE_AT), shape(lead + (8, GATE_AT))),
    ]
    scratch = [(length + RIM, GATE_AT), (4, length + 2 * RIM, GATE_AT)]
    args = (pre, rim, taps, par, segs, inverse, step, states)
    args += (d_gated, mixer, gain, pull, d_end)
    return call(back_kernel, lead, in_specs, outs, scratch, 60, args)


def passed_along(value, axis, steps):
    count = lax.axis_size(axis)
    first, last = (max(0, -steps), min(count, count - steps))
    return lax.ppermute(value, axis, [(source, source + steps) for source in range(first, last)])


def swapped(value, axis, bits):
    count = lax.axis_size(axis)
    return lax.ppermute(value, axis, [(place, place ^ bits) for place in range(count)])


def summed_everywhere(value):
    for axis in ("core", "px", "ctx", "tensor"):
        bits = 1
        while bits < lax.axis_size(axis):
            value = value + swapped(value, axis, bits)
            bits *= 2
    return value


def seg_ids(starts, spots):
    return jnp.sum((starts[:, None, :] <= spots[None, :, None]).astype(jnp.int32), axis=2) - 1


def rms_rows(values):
    return values * lax.rsqrt(jnp.mean(values * values, axis=-1, keepdims=True) + EPS_NORM)


def norm_scaled(values, gain):
    return rms_rows(values) * gain


def matmul(left, right):
    return lax.dot_general(left, right, NN, preferred_element_type=jnp.float32)


def matmul_left_t(left, right):
    return lax.dot_general(left, right, TN, preferred_element_type=jnp.float32)


def matmul_right_t(left, right):
    return lax.dot_general(left, right, NT, preferred_element_type=jnp.float32)


def apply_map(linear, state):
    return jnp.einsum("shij,shjv->shiv", linear, state, precision=FULL_ACCURACY)


def apply_map_t(linear, state):
    return jnp.einsum("shji,shjv->shiv", linear, state, precision=FULL_ACCURACY)


def dealt_by_sequence(own):
    lane, lanes = lax.axis_index("tensor"), lax.axis_size("tensor")
    each = own.shape[0] // lanes
    tokens = own.shape[1]
    result = jnp.zeros((each, tokens * lanes) + own.shape[2:], own.dtype)
    for bits in range(lanes):
        other = lane ^ bits
        part = lax.dynamic_slice_in_dim(own, other * each, each, 0)
        if bits:
            part = swapped(part, "tensor", bits)
        result = lax.dynamic_update_slice_in_dim(result, part, other * tokens, 1)
    return result


def dealt_by_tokens(rows):
    lane, lanes = lax.axis_index("tensor"), lax.axis_size("tensor")
    each, tokens = rows.shape[0], rows.shape[1] // lanes
    result = jnp.zeros((each * lanes, tokens) + rows.shape[2:], rows.dtype)
    for bits in range(lanes):
        other = lane ^ bits
        part = lax.dynamic_slice_in_dim(rows, other * tokens, tokens, 1)
        if bits:
            part = swapped(part, "tensor", bits)
        result = lax.dynamic_update_slice_in_dim(result, part, other * each, 0)
    return result


def with_partner(own):
    return jnp.concatenate([own, swapped(own, "core", 1)], 0)


def sum_with_partner(partial_sums):
    half = partial_sums.shape[0] // 2
    received = swapped(partial_sums[half:], "core", 1)
    return partial_sums[:half].astype(jnp.float32) + received.astype(jnp.float32)


SPREAD = ("tensor", "px", "ctx")


def gather_weights(halves_of_cols):
    core = lax.axis_index("core")
    first, second = halves_of_cols
    mine = jnp.where(core == 0, first, second)
    received = swapped(jnp.where(core == 0, second, first), "core", 1)
    rows, cols = mine.shape
    pair = jnp.stack(
        [jnp.where(core == 0, mine, received), jnp.where(core == 0, received, mine)]
    )
    full = lax.all_gather(pair.reshape(2 * rows, cols), SPREAD, axis=0, tiled=True)
    return full.reshape(tuple(lax.axis_size(axis) for axis in SPREAD) + (2, rows, cols))


def whole_rows(gathered, first, width):
    part = gathered[..., first : first + width]
    part = jnp.transpose(part, (1, 3, 2, 4, 0, 5))
    return part.reshape(-1, part.shape[4] * width)


def split_rows(grad, lanes):
    px, pieces = lax.axis_size("px"), lax.axis_size("ctx")
    rows = grad.shape[0] // (2 * px * pieces)
    shaped = grad.reshape(px, 2, pieces, rows, lanes, grad.shape[1] // lanes)
    return jnp.transpose(shaped, (4, 0, 2, 1, 3, 5))


def scatter_grads(parts):
    core = lax.axis_index("core")
    joined = jnp.concatenate(parts, -1)
    rows, cols = joined.shape[-2:]
    summed = lax.psum_scatter(
        joined.reshape(-1, cols), SPREAD, scatter_dimension=0, tiled=True
    )
    top, bottom = summed[:rows], summed[rows:]
    mine = jnp.where(core == 0, top, bottom)
    received = swapped(jnp.where(core == 0, bottom, top), "core", 1)
    first = jnp.where(core == 0, mine, received).astype(jnp.float32)
    second = jnp.where(core == 0, received, mine).astype(jnp.float32)
    return first, second


def padded_cols(array, width):
    return jnp.pad(array, ((0, 0), (0, width - array.shape[1])))


def up_to(value, step):
    return -(-value // step) * step


def shards(
    tokens,
    seg_starts,
    norm_gain,
    w_query,
    w_key,
    w_value,
    w_gate,
    w_alpha,
    w_beta,
    conv_query,
    conv_key,
    conv_value,
    a_log,
    dt_bias,
    out_gain,
    w_out,
    ffn_gain,
    w_ffn_gate,
    w_ffn_up,
    w_ffn_down,
    d_mixed,
):
    low = jnp.bfloat16
    core = lax.axis_index("core")
    lane = lax.axis_index("tensor")
    place = lax.axis_index("ctx")
    lanes = lax.axis_size("tensor")
    pieces = lax.axis_size("ctx")
    model = tokens.shape[2]
    length = tokens.shape[1] * lanes
    own_seqs = tokens.shape[0] // lanes
    seqs = 2 * own_seqs
    flat = seqs * length
    quarter_heads = w_alpha.shape[1]
    per_quarter = quarter_heads // 2
    heads = per_quarter * lanes
    units = w_ffn_gate.shape[1]
    half_units = units // 2
    wide = up_to(half_units, 128)
    val_cols = per_quarter * VAL
    count = length // CHUNK

    def head_block(number):
        key = slice(number * KEY, (number + 1) * KEY)
        val = slice(number * VAL, (number + 1) * VAL)
        one = slice(number, number + 1)
        parts = [w_query[:, key], w_key[:, key], w_value[:, val], w_gate[:, val]]
        return padded_cols(
            jnp.concatenate(parts + [w_alpha[:, one], w_beta[:, one]], 1), HEAD
        )

    def mix_half(half):
        numbers = range(half * per_quarter, (half + 1) * per_quarter)
        return jnp.concatenate([head_block(number) for number in numbers], 1)

    def rest_half(half):
        inner = slice(half * half_units, (half + 1) * half_units)
        outer = slice(half * val_cols, (half + 1) * val_cols)
        parts = [w_ffn_gate[:, inner], w_ffn_up[:, inner], w_ffn_down[inner].T]
        return jnp.concatenate(
            [padded_cols(part, wide) for part in parts] + [w_out[outer].T], 1
        )

    def of_heads(array, width):
        shaped = array.reshape(array.shape[0], lanes, 2, per_quarter * width)
        return jnp.where(core == 0, shaped[:, :, 0], shaped[:, :, 1]).reshape(
            array.shape[0], heads, width
        )

    mix_parts = gather_weights((mix_half(0), mix_half(1)))
    own = dealt_by_sequence(tokens).astype(jnp.float32)
    normed_own = (rms_rows(own) * norm_gain).astype(low)
    normed = with_partner(normed_own).reshape(flat, model)
    rest_parts = gather_weights((rest_half(0), rest_half(1)))
    w_mix = whole_rows(mix_parts, 0, per_quarter * HEAD)
    pre = matmul(normed, w_mix).reshape(seqs, length, heads * HEAD)
    rim = passed_along(pre[:, length - RIM :], "ctx", 1)
    starts_own = lax.dynamic_slice_in_dim(seg_starts, lane * own_seqs, own_seqs, 0)
    starts = with_partner(starts_own.astype(jnp.float32)).astype(jnp.int32)
    base = place * length
    seg_ext = seg_ids(starts, base + jnp.arange(-3, length, dtype=jnp.int32))
    segs = jnp.stack(
        [seg_ext[:, 3 - n : 3 - n + length].reshape(seqs, count, CHUNK) for n in range(4)], 2
    ).astype(jnp.float32)
    segs = jnp.pad(segs, ((0, 0), (0, 0), (0, 4), (0, 0)))
    taps = jnp.concatenate(
        [of_heads(conv_query, KEY), of_heads(conv_key, KEY), of_heads(conv_value, VAL)], 2
    ).reshape(4, heads * GATE_AT)
    par = jnp.stack(
        [of_heads(-jnp.exp(a_log)[None], 1)[0, :, 0], of_heads(dt_bias[None], 1)[0, :, 0]], 1
    )
    par = jnp.broadcast_to(
        jnp.pad(par, ((0, 0), (0, 6)))[:, :, None], (heads, 8, 128)
    )
    gain_row = out_gain[None]
    inverse, step, push, read, base_out, end_map, end_push = run_front(
        pre, rim, taps, par, segs
    )
    cot_own = dealt_by_sequence(d_mixed)
    cot = with_partner(cot_own).reshape(flat, model)
    state_in = passed_along(end_push, "ctx", 1)
    if pieces > 2:
        state_in = lax.fori_loop(
            0,
            pieces - 2,
            lambda turn, state: passed_along(apply_map(end_map, state) + end_push, "ctx", 1),
            state_in,
        )
    states, mixer, gated = run_output(state_in, step, push, read, base_out, pre, gain_row)
    gated_flat = gated.reshape(flat, heads * VAL)
    w_pair = jnp.concatenate(
        [whole_rows(rest_parts, 0, wide), whole_rows(rest_parts, wide, wide)], 1
    )
    w_down_t = whole_rows(rest_parts, 2 * wide, wide)
    w_out_t = whole_rows(rest_parts, 3 * wide, val_cols)
    attn_part = matmul_right_t(gated_flat, w_out_t).astype(low)
    middle = own + sum_with_partner(attn_part.reshape(seqs, length, model))
    normed_two_own = (rms_rows(middle) * ffn_gain).astype(low)
    normed_two = with_partner(normed_two_own).reshape(flat, model)
    width = lanes * wide
    pair = matmul(normed_two, w_pair)
    gate_pre, up_pre = pair[:, :width], pair[:, width:]
    sigma = jax.nn.sigmoid(gate_pre)
    hidden = (gate_pre * sigma * up_pre).astype(low)
    d_hidden = matmul(cot, w_down_t)
    d_gate_pre = (d_hidden * up_pre * sigma * (1.0 + gate_pre * (1.0 - sigma))).astype(low)
    d_up_pre = (d_hidden * gate_pre * sigma).astype(low)
    d_pair = jnp.concatenate([d_gate_pre, d_up_pre], 1)
    ffn_terms = matmul_right_t(d_pair, w_pair).astype(low)
    d_normed_two = sum_with_partner(ffn_terms.reshape(seqs, length, model))
    _, norm_two_back = jax.vjp(norm_scaled, middle, ffn_gain)
    d_middle_part, grad_ffn_gain = norm_two_back(d_normed_two)
    d_middle = cot_own.astype(jnp.float32) + d_middle_part
    d_branch = with_partner(d_middle.astype(low)).reshape(flat, model)
    d_gated = matmul(d_branch, w_out_t).reshape(seqs, length, heads * VAL)
    pull, d_start = run_pull(d_gated, mixer, pre, gain_row, step, read)
    d_end = passed_along(d_start, "ctx", -1)
    if pieces > 2:
        d_end = lax.fori_loop(
            0,
            pieces - 2,
            lambda turn, state: passed_along(apply_map_t(end_map, state) + d_start, "ctx", -1),
            d_end,
        )
    grad_pair = matmul_left_t(normed_two, d_pair).astype(low)
    rest_first, rest_second = scatter_grads(
        [
            split_rows(grad_pair[:, :width], lanes),
            split_rows(grad_pair[:, width:], lanes),
            split_rows(matmul_left_t(cot, hidden).astype(low), lanes),
            split_rows(matmul_left_t(d_branch, gated_flat).astype(low), lanes),
        ]
    )
    ffn_part = matmul_right_t(hidden, w_down_t).astype(low)
    ffn_own = sum_with_partner(ffn_part.reshape(seqs, length, model))
    mixed = dealt_by_tokens((middle + ffn_own).astype(low))
    d_all, d_rim, d_small = run_back(
        pre, rim, taps, par, segs, inverse, step, states, d_gated, mixer, gain_row, pull, d_end
    )
    back_rim = passed_along(d_rim, "ctx", -1).reshape(seqs, RIM, heads, GATE_AT)
    back_rim = jnp.pad(back_rim, ((0, 0),) * 3 + ((0, HEAD - GATE_AT),))
    tail = d_all[:, length - RIM :].astype(jnp.float32) + back_rim.reshape(seqs, RIM, -1)
    d_all = lax.dynamic_update_slice(d_all, tail.astype(low), (0, length - RIM, 0))
    d_all = d_all.reshape(flat, heads * HEAD)
    d_normed = matmul_right_t(d_all, w_mix).astype(low)
    own_d_normed = sum_with_partner(d_normed.reshape(seqs, length, model))
    mix_first, mix_second = scatter_grads(
        [split_rows(matmul_left_t(normed, d_all).astype(low), lanes)]
    )
    _, norm_back = jax.vjp(norm_scaled, own, norm_gain)
    d_own, grad_norm_gain = norm_back(own_d_normed)
    grad_tokens = dealt_by_tokens((d_middle + d_own).astype(low)).astype(jnp.float32)

    small = jnp.sum(d_small, axis=0)

    def placed(part):
        rows, _, each = part.shape
        shaped = part.reshape(rows, lanes, 1, per_quarter * each)
        empty = jnp.zeros_like(shaped)
        both = jnp.where(
            core == 0,
            jnp.concatenate([shaped, empty], 2),
            jnp.concatenate([empty, shaped], 2),
        )
        return both.reshape(-1)

    conv_parts = jnp.transpose(small[:, :4], (1, 0, 2))
    items = [
        grad_ffn_gain,
        placed(conv_parts[..., :KEY]),
        placed(conv_parts[..., KEY : 2 * KEY]),
        placed(conv_parts[..., 2 * KEY :]),
        jnp.sum(small[:, 4, :VAL], axis=0),
        placed(small[None, :, 5, :1]),
        placed(small[None, :, 6, :1]),
    ]
    sizes = [item.shape[0] for item in items]
    total = up_to(sum(sizes), 1024)
    joined = jnp.concatenate(items + [jnp.zeros((total - sum(sizes),), jnp.float32)])
    joined = summed_everywhere(joined.reshape(-1, 128)).reshape(-1)
    norm_sum = summed_everywhere(grad_norm_gain.reshape(8, -1)).reshape(-1)
    ends = [sum(sizes[: n + 1]) for n in range(len(sizes))]
    sums = [joined[end - size : end] for size, end in zip(sizes, ends)]

    def mix_cols(first, width):
        halves_of = [
            half.reshape(half.shape[0], per_quarter, HEAD)[:, :, first : first + width].reshape(
                half.shape[0], -1
            )
            for half in (mix_first, mix_second)
        ]
        return jnp.concatenate(halves_of, 1)

    def rest_cols(first, width):
        return jnp.concatenate(
            [half[:, first : first + width] for half in (rest_first, rest_second)], 1
        )

    return (
        mixed,
        grad_tokens,
        norm_sum,
        mix_cols(0, KEY),
        mix_cols(KEY, KEY),
        mix_cols(2 * KEY, VAL),
        mix_cols(GATE_AT, VAL),
        mix_cols(AB_AT, 1),
        mix_cols(AB_AT + 1, 1),
        sums[1].reshape(4, -1),
        sums[2].reshape(4, -1),
        sums[3].reshape(4, -1),
        sums[5],
        sums[6],
        sums[4],
        rest_cols(3 * wide, val_cols).T,
        sums[0],
        rest_cols(0, half_units),
        rest_cols(wide, half_units),
        rest_cols(2 * wide, half_units).T,
    )


def solution(mesh):
    sizes = tuple(mesh.shape[axis] for axis in ("dp", "ctx", "tensor"))
    fine = Mesh(
        mesh.devices.reshape((sizes[0] // 2, 2) + sizes[1:]), ("px", "core", "ctx", "tensor")
    )
    dp = ("px", "core")
    rows = P(("px", "core", "ctx"), "tensor")
    cols = P("tensor", ("px", "core", "ctx"))
    own = P(dp, ("ctx", "tensor"), None)
    return jax.shard_map(
        shards,
        mesh=fine,
        in_specs=(own, P(dp, None), P())
        + (rows,) * 6
        + (P(),) * 6
        + (cols, P(), rows, rows, cols, own),
        out_specs=(own, own, P())
        + (rows,) * 6
        + (P(),) * 6
        + (cols, P(), rows, rows, cols),
        check_vma=False,
    )
```

```python
from functools import partial

import jax
import jax.numpy as jnp
from jax import lax
from jax.experimental import pallas as pl
from jax.experimental.pallas import tpu as pltpu
from jax.sharding import Mesh, PartitionSpec as P

CHUNK = 128
RIM = 8
EPS_NORM = 1e-05
EPS_UNIT = 1e-06
FULL_ACCURACY = lax.Precision.HIGHEST
NN = (((1,), (0,)), ((), ()))
NT = (((1,), (1,)), ((), ()))
TN = (((0,), (0,)), ((), ()))


def dot_low(left, right, dims):
    return lax.dot_general(
        left.astype(jnp.bfloat16),
        right.astype(jnp.bfloat16),
        dims,
        preferred_element_type=jnp.float32,
    )


def halves(value):
    high = value.astype(jnp.bfloat16)
    return high, (value - high.astype(jnp.float32)).astype(jnp.bfloat16)


def dot_split(left, right, dims):
    left_high, left_low = halves(left)
    right_high, right_low = halves(right)
    total = lax.dot_general(left_high, right_high, dims, preferred_element_type=jnp.float32)
    total += lax.dot_general(left_high, right_low, dims, preferred_element_type=jnp.float32)
    return total + lax.dot_general(left_low, right_high, dims, preferred_element_type=jnp.float32)


def sigmoid(value):
    return 1.0 / (1.0 + jnp.exp(-value))


def positions():
    row = lax.broadcasted_iota(jnp.int32, (CHUNK, CHUNK), 0)
    col = lax.broadcasted_iota(jnp.int32, (CHUNK, CHUNK), 1)
    return row, col


def unit_lower_inverses(lowers):
    row, col = positions()
    eye = (row == col).astype(jnp.float32)
    diag = [jnp.where(row // 8 == col // 8, low, 0.0) for low in lowers]
    result = [eye - d for d in diag]
    power = [dot_split(d, d, NN) for d in diag]
    result = [x + dot_split(x, p, NN) for x, p in zip(result, power)]
    power = [dot_split(p, p, NN) for p in power]
    result = [x + dot_split(x, p, NN) for x, p in zip(result, power)]
    size = 8
    while size < CHUNK:
        across = (row // (2 * size) == col // (2 * size)) & (row // size != col // size)
        mixed = [dot_split(jnp.where(across, low, 0.0), x, NN) for low, x in zip(lowers, result)]
        result = [x - dot_split(x, m, NN) for x, m in zip(result, mixed)]
        size *= 2
    return result


KEY = 128
VAL = 256
GATE_AT = 2 * KEY + VAL
AB_AT = GATE_AT + VAL
HEAD = AB_AT + 128
VMEM_BYTES = 48 * 2**20


def thirds(value):
    high = value.astype(jnp.bfloat16)
    rest = value - high.astype(jnp.float32)
    middle = rest.astype(jnp.bfloat16)
    return high, middle, (rest - middle.astype(jnp.float32)).astype(jnp.bfloat16)


def dot_ones(ones, value, dims):
    left = ones.astype(jnp.bfloat16)
    return sum(
        lax.dot_general(left, part, dims, preferred_element_type=jnp.float32)
        for part in thirds(value)
    )


def unit(values):
    scale = lax.rsqrt(jnp.sum(values * values, axis=-1, keepdims=True) + EPS_UNIT)
    return values * scale, scale


def last_value(column):
    return column[CHUNK - 1 : CHUNK, :]


def spread_lanes(column):
    return jnp.broadcast_to(column, (CHUNK, CHUNK))


def chunk_parts(pre, par, segs, index):
    rows = slice(index * CHUNK, (index + 1) * CHUNK)
    row, col = positions()
    tile = segs[0, index]
    columns = jnp.concatenate([tile, jnp.zeros((CHUNK - 8, CHUNK), jnp.float32)], axis=0).T
    seg = columns[:, 0:1]
    masks = [(seg == columns[:, n : n + 1]).astype(jnp.float32) for n in range(1, 4)]
    shifted = pre[0, rows, AB_AT : AB_AT + 1] + par[0, 1:2, 0:1]
    strength = sigmoid(pre[0, rows, AB_AT + 1 : AB_AT + 2])
    soft = jnp.maximum(shifted, 0.0) + jnp.log1p(jnp.exp(-jnp.abs(shifted)))
    decay = par[0, 0:1, 0:1] * soft
    lower = (row >= col).astype(jnp.float32)
    cumul = dot_ones(lower, spread_lanes(decay), NN)
    allowed = (row >= col) & (seg == tile[0:1, :])
    within = jnp.where(allowed, jnp.exp(jnp.minimum(cumul - cumul.T, 0.0)), 0.0)
    cum = cumul[:, 0:1]
    opening = jnp.where(seg == tile[1:2, 0:1], jnp.exp(cum), 0.0)
    closing = jnp.where(
        seg == tile[0:1, CHUNK - 1 :], jnp.exp(jnp.minimum(last_value(cum) - cum, 0.0)), 0.0
    )
    return dict(
        rows=rows,
        masks=masks,
        shifted=shifted,
        decay=decay,
        strength=strength,
        opening=opening,
        closing=closing,
        within=within,
    )


def fill_ext(ext, rim, pre):
    ext[0:RIM, :] = rim[0, :, :GATE_AT]
    ext[RIM:, :] = pre[0, :, :GATE_AT]


def conv_chunk(ext, taps, part):
    first = RIM + part["rows"].start
    total = taps[0:1, :] * ext[first : first + CHUNK, :]
    for offset in range(1, 4):
        shifted = ext[first - offset : first - offset + CHUNK, :]
        total = total + taps[offset : offset + 1, :] * shifted * part["masks"][offset - 1]
    return total


def split_qkv(array):
    return array[:, :KEY], array[:, KEY : 2 * KEY], array[:, 2 * KEY :]

GROUP = 4


def front_terms(pre, ext, taps, par, segs, first, last):
    row, col = positions()
    eye = (row == col).astype(jnp.float32)
    parts = [chunk_parts(pre, par, segs, n) for n in range(first, last)]
    convs = [conv_chunk(ext, taps, p) for p in parts]
    acts = [split_qkv(c * sigmoid(c)) for c in convs]
    queries = [unit(a[0])[0] * (float(KEY) ** -0.5) for a in acts]
    keys = [unit(a[1])[0] for a in acts]
    inner = [dot_split(k, k, NT) for k in keys]
    lowers = [
        jnp.where(row > col, p["strength"] * p["within"] * i, 0.0) for p, i in zip(parts, inner)
    ]
    inverses = unit_lower_inverses(lowers)
    scores = [dot_low(q, k, NT) * p["within"] for q, k, p in zip(queries, keys, parts)]
    known = [
        dot_low(t, p["strength"] * a[2], NN) for t, p, a in zip(inverses, parts, acts)
    ]
    write = [
        dot_low(t, p["strength"] * p["opening"] * k, NN)
        for t, p, k in zip(inverses, parts, keys)
    ]
    closed = [p["closing"] * k for p, k in zip(parts, keys)]
    steps = [
        last_value(p["opening"]) * eye - dot_low(c, w, TN)
        for p, c, w in zip(parts, closed, write)
    ]
    pushes = [dot_low(c, u, TN) for c, u in zip(closed, known)]
    reads = [
        p["opening"] * q - dot_low(s, w, NN)
        for p, q, s, w in zip(parts, queries, scores, write)
    ]
    bases = [dot_low(s, u, NN) for s, u in zip(scores, known)]
    return inverses, steps, pushes, reads, bases


def write_output(state, base, read, pre, gain, rows, mixer_out, gated_out):
    mixer = base + dot_low(read, state, NN)
    mixer_out[0, 0, rows, :] = mixer
    scale = lax.rsqrt(jnp.mean(mixer * mixer, axis=-1, keepdims=True) + EPS_NORM)
    gate = pre[0, rows, GATE_AT:AB_AT]
    gated_out[0, rows, :] = (mixer * scale * gain[...] * gate * sigmoid(gate)).astype(
        jnp.bfloat16
    )


def chunk_rows(number):
    return slice(number * CHUNK, (number + 1) * CHUNK)


def front_kernel(
    pre, rim, taps, par, segs,
    inverse_out, step_out, push_out, read_out, base_out, end_map, end_push,
    ext,
):
    count = pre.shape[1] // CHUNK
    fill_ext(ext, rim, pre)
    total_map = total_push = None
    for first in range(0, count, GROUP):
        last = min(count, first + GROUP)
        terms = front_terms(pre, ext, taps, par, segs, first, last)
        for n in range(first, last):
            rows = chunk_rows(n)
            inverse, step, push, read, base = (term[n - first] for term in terms)
            inverse_out[0, 0, rows, :] = inverse
            step_out[0, 0, rows, :] = step
            push_out[0, 0, rows, :] = push
            read_out[0, 0, rows, :] = read
            base_out[0, 0, rows, :] = base
            if n:
                total_push = dot_low(step, total_push, NN) + push
                total_map = dot_low(step, total_map, NN)
            else:
                total_map, total_push = step, push
    end_map[0, 0] = total_map
    end_push[0, 0] = total_push


def whole_kernel(
    pre, rim, taps, par, segs, gain,
    inverse_out, step_out, read_out, states_out, mixer_out, gated_out,
    ext,
):
    count = pre.shape[1] // CHUNK
    fill_ext(ext, rim, pre)
    state = jnp.zeros((KEY, VAL), jnp.float32)
    for first in range(0, count, GROUP):
        last = min(count, first + GROUP)
        terms = front_terms(pre, ext, taps, par, segs, first, last)
        for n in range(first, last):
            rows = chunk_rows(n)
            inverse, step, push, read, base = (term[n - first] for term in terms)
            inverse_out[0, 0, rows, :] = inverse
            step_out[0, 0, rows, :] = step
            read_out[0, 0, rows, :] = read
            states_out[0, 0, rows, :] = state
            write_output(state, base, read, pre, gain, rows, mixer_out, gated_out)
            state = dot_low(step, state, NN) + push


def output_kernel(
    state_in, step, push, read, base, pre, gain, states_out, mixer_out, gated_out
):
    count = step.shape[2] // CHUNK
    state = state_in[0, 0]
    for n in range(count):
        rows = chunk_rows(n)
        states_out[0, 0, rows, :] = state
        write_output(
            state, base[0, 0, rows, :], read[0, 0, rows, :], pre, gain, rows, mixer_out, gated_out
        )
        if n < count - 1:
            state = dot_low(step[0, 0, rows, :], state, NN) + push[0, 0, rows, :]


def mixer_back(d_gated, mixer_in, pre, gain, rows):
    mixer = mixer_in[0, 0, rows, :]
    scale = lax.rsqrt(jnp.mean(mixer * mixer, axis=-1, keepdims=True) + EPS_NORM)
    normed = mixer * scale
    gate = pre[0, rows, GATE_AT:AB_AT]
    sig = sigmoid(gate)
    grad = d_gated[0, rows, :]
    through = grad * gate * sig
    d_normed = through * gain[...]
    d_mixer = scale * (d_normed - normed * jnp.mean(d_normed * normed, axis=-1, keepdims=True))
    d_gate = grad * normed * gain[...] * sig * (1.0 + gate * (1.0 - sig))
    return d_mixer, d_gate, jnp.sum(through * normed, axis=0, keepdims=True)


def pull_kernel(d_gated, mixer_in, pre, gain, step, read, pull_out, start_out):
    count = step.shape[2] // CHUNK
    carried = None
    for n in reversed(range(count)):
        rows = slice(n * CHUNK, (n + 1) * CHUNK)
        d_mixer = mixer_back(d_gated, mixer_in, pre, gain, rows)[0]
        pull = dot_low(read[0, 0, rows, :], d_mixer, TN)
        pull_out[0, 0, rows, :] = pull
        if carried is None:
            carried = pull
        else:
            carried = dot_low(step[0, 0, rows, :], carried, TN) + pull
    start_out[0, 0] = carried


def back_kernel(alone, pre, rim, taps, par, segs, inverse, step, states, d_gated, mixer_in, gain, *refs):
    if alone:
        read, d_all_out, d_rim_out, d_small_out, ext, pad = refs
    else:
        pull, d_end, d_all_out, d_rim_out, d_small_out, ext, pad = refs
    length = pre.shape[1]
    count = length // CHUNK
    fill_ext(ext, rim, pre)
    row, col = positions()
    lane = col
    last_row = lax.broadcasted_iota(jnp.int32, (CHUNK, 1), 0) == CHUNK - 1
    lower = (row >= col).astype(jnp.float32)
    d_states = [None] * count
    d_states[count - 1] = jnp.zeros((KEY, VAL), jnp.float32) if alone else d_end[0, 0]
    for n in reversed(range(1, count)):
        block = chunk_rows(n)
        if alone:
            d_mixer = mixer_back(d_gated, mixer_in, pre, gain, block)[0]
            back = dot_low(read[0, 0, block, :], d_mixer, TN)
        else:
            back = pull[0, 0, block, :]
        d_states[n - 1] = dot_low(step[0, 0, block, :], d_states[n], TN) + back
    pad[:, 0:RIM, :] = jnp.zeros((4, RIM, GATE_AT), jnp.float32)
    pad[:, RIM + length :, :] = jnp.zeros((4, RIM, GATE_AT), jnp.float32)
    d_gain = jnp.zeros((1, VAL), jnp.float32)
    d_log = jnp.zeros((1, 1), jnp.float32)
    d_bias = jnp.zeros((1, 1), jnp.float32)
    d_taps = [jnp.zeros((1, GATE_AT), jnp.float32) for _ in range(4)]
    for n in range(count):
        part = chunk_parts(pre, par, segs, n)
        block, within = part["rows"], part["within"]
        strength, opening, closing = part["strength"], part["opening"], part["closing"]
        conv = conv_chunk(ext, taps, part)
        sig = sigmoid(conv)
        act_q, act_k, value = split_qkv(conv * sig)
        unit_q, scale_q = unit(act_q)
        key, scale_k = unit(act_k)
        query = unit_q * (float(KEY) ** -0.5)
        state, d_state = states[0, 0, block, :], d_states[n]
        solve = inverse[0, 0, block, :]
        grad, d_gate, d_gain_part = mixer_back(d_gated, mixer_in, pre, gain, block)
        d_gain = d_gain + d_gain_part
        rest = value - opening * dot_low(key, state, NN)
        update = dot_low(solve, strength * rest, NN)
        scores = dot_low(query, key, NT) * within
        inner = dot_low(key, key, NT) * within
        closed = closing * key
        d_update = dot_low(scores, grad, TN) + dot_low(closed, d_state, NN)
        d_right = dot_low(solve, d_update, TN)
        d_scores = dot_low(grad, update, NT)
        d_lower = jnp.where(row > col, -dot_low(d_right, update, NT), 0.0)
        d_plain = d_scores * within
        d_inner = d_lower * strength * within
        read_back = dot_low(grad, state, NT)
        known_back = -dot_low(strength * d_right, state, NT)
        closed_back = dot_low(update, d_state, NT)
        d_query = opening * read_back + dot_low(d_plain, key, NN)
        d_key = (
            dot_low(d_plain, query, TN)
            + dot_low(d_inner, key, NN)
            + dot_low(d_inner, key, TN)
            + opening * known_back
            + closing * closed_back
        )
        lower_parts = d_lower * inner
        d_strength = jnp.sum(lower_parts, axis=1, keepdims=True) + jnp.sum(
            d_right * rest, axis=1, keepdims=True
        )
        spread = d_scores * scores + strength * lower_parts
        d_opening = jnp.sum(query * read_back + key * known_back, axis=1, keepdims=True)
        d_closing = jnp.sum(key * closed_back, axis=1, keepdims=True) * closing
        through = jnp.sum(
            jnp.sum(state * d_state, axis=1, keepdims=True), axis=0, keepdims=True
        )
        end_sum = jnp.sum(d_closing, axis=0, keepdims=True) + through * last_value(opening)
        d_cumul = (
            jnp.sum(spread, axis=1, keepdims=True)
            + d_opening * opening
            - d_closing
            + jnp.where(last_row, end_sum, 0.0)
        )
        down = spread_lanes(jnp.sum(spread, axis=0, keepdims=True)).T
        d_decay = dot_ones(lower, spread_lanes(d_cumul) - down, TN)[:, 0:1]
        d_alpha = d_decay * par[0, 0:1, 0:1] * sigmoid(part["shifted"])
        d_beta = d_strength * strength * (1.0 - strength)
        d_log = d_log + jnp.sum(d_decay * part["decay"], axis=0, keepdims=True)
        d_bias = d_bias + jnp.sum(d_alpha, axis=0, keepdims=True)
        d_all_out[0, block, GATE_AT:AB_AT] = d_gate.astype(jnp.bfloat16)
        d_all_out[0, block, AB_AT:] = jnp.where(
            lane == 0, d_alpha, jnp.where(lane == 1, d_beta, 0.0)
        ).astype(jnp.bfloat16)
        d_query = d_query * (float(KEY) ** -0.5)
        d_act = jnp.concatenate(
            [
                scale_q * (d_query - unit_q * jnp.sum(unit_q * d_query, axis=-1, keepdims=True)),
                scale_k * (d_key - key * jnp.sum(key * d_key, axis=-1, keepdims=True)),
                strength * d_right,
            ],
            axis=1,
        )
        d_conv = d_act * sig * (1.0 + conv * (1.0 - sig))
        first = RIM + block.start
        for offset in range(4):
            masked = d_conv if offset == 0 else d_conv * part["masks"][offset - 1]
            shifted = ext[first - offset : first - offset + CHUNK, :]
            d_taps[offset] = d_taps[offset] + jnp.sum(masked * shifted, axis=0, keepdims=True)
            pad[offset, first : first + CHUNK, :] = masked * taps[offset : offset + 1, :]
    d_rim = pad[0, 0:RIM, :]
    for offset in range(1, 4):
        d_rim = d_rim + pad[offset, offset : offset + RIM, :]
    d_rim_out[0] = d_rim
    for n in range(count):
        first = RIM + n * CHUNK
        total = pad[0, first : first + CHUNK, :]
        for offset in range(1, 4):
            total = total + pad[offset, first + offset : first + offset + CHUNK, :]
        d_all_out[0, n * CHUNK : (n + 1) * CHUNK, :GATE_AT] = total.astype(jnp.bfloat16)
    for offset in range(4):
        d_small_out[0, 0, offset : offset + 1, :] = d_taps[offset]
    d_small_out[0, 0, 4:5, :] = jnp.concatenate([d_gain, d_gain], axis=1)
    d_small_out[0, 0, 5:6, :] = jnp.broadcast_to(d_log, (1, GATE_AT))
    d_small_out[0, 0, 6:7, :] = jnp.broadcast_to(d_bias, (1, GATE_AT))
    d_small_out[0, 0, 7:8, :] = jnp.zeros((1, GATE_AT), jnp.float32)


def per_head(*tail):
    return pl.BlockSpec((1, 1) + tail, lambda s, h: (s, h) + (0,) * len(tail))


def lanes_at(rows, width):
    return pl.BlockSpec((1, rows, width), lambda s, h: (s, 0, h))


def front_specs(length):
    return [
        lanes_at(length, HEAD),
        lanes_at(RIM, HEAD),
        pl.BlockSpec((4, GATE_AT), lambda s, h: (0, h)),
        pl.BlockSpec((1, 8, 128), lambda s, h: (h, 0, 0)),
        pl.BlockSpec((1, length // CHUNK, 8, CHUNK), lambda s, h: (s, 0, 0, 0)),
    ]


def gain_spec():
    return pl.BlockSpec((1, VAL), lambda s, h: (0, 0))


def shape(dims, kind=jnp.float32):
    return jax.ShapeDtypeStruct(dims, kind)


def call(kernel, lead, in_specs, outs, scratch, units, args):
    length = args[0].shape[1] if args[0].ndim == 3 else args[1].shape[2]
    flops = lead[0] * lead[1] * length * 128 * 128 * 2 * units
    return pl.pallas_call(
        kernel,
        grid=lead,
        in_specs=in_specs,
        out_specs=[spec for spec, _ in outs],
        out_shape=[kind for _, kind in outs],
        scratch_shapes=[pltpu.VMEM(dims, jnp.float32) for dims in scratch],
        compiler_params=pltpu.CompilerParams(vmem_limit_bytes=VMEM_BYTES),
        cost_estimate=pl.CostEstimate(
            flops=flops, bytes_accessed=flops // 100, transcendentals=0
        ),
    )(*args)


def run_front(pre, rim, taps, par, segs):
    seqs, length, wide = pre.shape
    lead = (seqs, wide // HEAD)
    widths = (KEY, KEY, VAL, KEY, VAL)
    outs = [(per_head(length, width), shape(lead + (length, width))) for width in widths]
    outs += [(per_head(KEY, width), shape(lead + (KEY, width))) for width in (KEY, VAL)]
    return call(
        front_kernel,
        lead,
        front_specs(length),
        outs,
        [(length + RIM, GATE_AT)],
        60,
        (pre, rim, taps, par, segs),
    )


def run_output(state_in, step, push, read, base, pre, gain):
    seqs, heads, length, _ = step.shape
    lead = (seqs, heads)
    in_specs = [per_head(KEY, VAL)]
    in_specs += [per_head(length, width) for width in (KEY, VAL, KEY, VAL)]
    in_specs += [lanes_at(length, HEAD), gain_spec()]
    outs = [
        (per_head(length, VAL), shape(lead + (length, VAL))),
        (per_head(length, VAL), shape(lead + (length, VAL))),
        (lanes_at(length, VAL), shape((seqs, length, heads * VAL), jnp.bfloat16)),
    ]
    args = (state_in, step, push, read, base, pre, gain)
    return call(output_kernel, lead, in_specs, outs, [], 15, args)


def run_pull(d_gated, mixer, pre, gain, step, read):
    seqs, heads, length, _ = step.shape
    lead = (seqs, heads)
    in_specs = [lanes_at(length, VAL), per_head(length, VAL), lanes_at(length, HEAD)]
    in_specs += [gain_spec(), per_head(length, KEY), per_head(length, KEY)]
    outs = [
        (per_head(length, VAL), shape(lead + (length, VAL))),
        (per_head(KEY, VAL), shape(lead + (KEY, VAL))),
    ]
    return call(
        pull_kernel, lead, in_specs, outs, [], 15, (d_gated, mixer, pre, gain, step, read)
    )


def run_whole(pre, rim, taps, par, segs, gain):
    seqs, length, wide = pre.shape
    heads = wide // HEAD
    lead = (seqs, heads)
    widths = (KEY, KEY, KEY, VAL, VAL)
    outs = [(per_head(length, width), shape(lead + (length, width))) for width in widths]
    outs.append((lanes_at(length, VAL), shape((seqs, length, heads * VAL), jnp.bfloat16)))
    return call(
        whole_kernel,
        lead,
        front_specs(length) + [gain_spec()],
        outs,
        [(length + RIM, GATE_AT)],
        70,
        (pre, rim, taps, par, segs, gain),
    )


def run_back(pre, rim, taps, par, segs, inverse, step, states, d_gated, mixer, gain, *ends):
    seqs, length, wide = pre.shape
    heads = wide // HEAD
    lead = (seqs, heads)
    alone = len(ends) == 1
    in_specs = front_specs(length)
    in_specs += [per_head(length, width) for width in (KEY, KEY, VAL)]
    in_specs += [lanes_at(length, VAL), per_head(length, VAL), gain_spec()]
    in_specs += [per_head(length, KEY)] if alone else [per_head(length, VAL), per_head(KEY, VAL)]
    outs = [
        (lanes_at(length, HEAD), shape((seqs, length, wide), jnp.bfloat16)),
        (lanes_at(RIM, GATE_AT), shape((seqs, RIM, heads * GATE_AT))),
        (per_head(8, GATE_AT), shape(lead + (8, GATE_AT))),
    ]
    scratch = [(length + RIM, GATE_AT), (4, length + 2 * RIM, GATE_AT)]
    args = (pre, rim, taps, par, segs, inverse, step, states)
    args += (d_gated, mixer, gain) + ends
    return call(partial(back_kernel, alone), lead, in_specs, outs, scratch, 60, args)


def passed_along(value, axis, steps):
    count = lax.axis_size(axis)
    first, last = (max(0, -steps), min(count, count - steps))
    return lax.ppermute(value, axis, [(source, source + steps) for source in range(first, last)])


def swapped(value, axis, bits):
    count = lax.axis_size(axis)
    return lax.ppermute(value, axis, [(place, place ^ bits) for place in range(count)])


def summed_everywhere(value):
    for axis in ("core", "px", "cg", "cl", "tensor"):
        bits = 1
        while bits < lax.axis_size(axis):
            value = value + swapped(value, axis, bits)
            bits *= 2
    return value


def seg_ids(starts, spots):
    return jnp.sum((starts[:, None, :] <= spots[None, :, None]).astype(jnp.int32), axis=2) - 1


def rms_rows(values):
    return values * lax.rsqrt(jnp.mean(values * values, axis=-1, keepdims=True) + EPS_NORM)


def norm_scaled(values, gain):
    return rms_rows(values) * gain


def matmul(left, right):
    return lax.dot_general(left, right, NN, preferred_element_type=jnp.float32)


def matmul_left_t(left, right):
    return lax.dot_general(left, right, TN, preferred_element_type=jnp.float32)


def matmul_right_t(left, right):
    return lax.dot_general(left, right, NT, preferred_element_type=jnp.float32)


def apply_map(linear, state):
    return jnp.einsum("shij,shjv->shiv", linear, state, precision=FULL_ACCURACY)


def apply_map_t(linear, state):
    return jnp.einsum("shji,shjv->shiv", linear, state, precision=FULL_ACCURACY)


def dealt_by_sequence(own):
    lane, lanes = lax.axis_index("tensor"), lax.axis_size("tensor")
    each = own.shape[0] // lanes
    tokens = own.shape[1]
    result = jnp.zeros((each, tokens * lanes) + own.shape[2:], own.dtype)
    for bits in range(lanes):
        other = lane ^ bits
        part = lax.dynamic_slice_in_dim(own, other * each, each, 0)
        if bits:
            part = swapped(part, "tensor", bits)
        result = lax.dynamic_update_slice_in_dim(result, part, other * tokens, 1)
    return result


def dealt_by_tokens(rows):
    lane, lanes = lax.axis_index("tensor"), lax.axis_size("tensor")
    each, tokens = rows.shape[0], rows.shape[1] // lanes
    result = jnp.zeros((each * lanes, tokens) + rows.shape[2:], rows.dtype)
    for bits in range(lanes):
        other = lane ^ bits
        part = lax.dynamic_slice_in_dim(rows, other * tokens, tokens, 1)
        if bits:
            part = swapped(part, "tensor", bits)
        result = lax.dynamic_update_slice_in_dim(result, part, other * each, 0)
    return result


def with_partner(own):
    return jnp.concatenate([own, swapped(own, "core", 1)], 0)


def with_group(own):
    side = lax.axis_index("cl")
    tokens = own.shape[1]
    both = jnp.zeros((own.shape[0], 2 * tokens) + own.shape[2:], own.dtype)
    both = lax.dynamic_update_slice_in_dim(both, own, side * tokens, 1)
    both = lax.dynamic_update_slice_in_dim(
        both, swapped(own, "cl", 1), (1 - side) * tokens, 1
    )
    return with_partner(both)


def sum_in_group(partial_sums):
    side = lax.axis_index("cl")
    half = partial_sums.shape[0] // 2
    received = swapped(partial_sums[half:], "core", 1)
    both = (partial_sums[:half].astype(jnp.float32) + received.astype(jnp.float32)).astype(
        partial_sums.dtype
    )
    tokens = both.shape[1] // 2
    mine = lax.dynamic_slice_in_dim(both, side * tokens, tokens, 1)
    other = lax.dynamic_slice_in_dim(both, (1 - side) * tokens, tokens, 1)
    return mine.astype(jnp.float32) + swapped(other, "cl", 1).astype(jnp.float32)


SPREAD = ("tensor", "px", "cg")


def traded(value):
    lanes = lax.axis_size("tensor")
    pairs = [
        (side * lanes + lane, (1 - side) * lanes + (lane ^ 1))
        for side in range(2)
        for lane in range(lanes)
        if lane % 2 != side
    ]
    received = lax.ppermute(value, ("cl", "tensor"), pairs)
    stays = lax.axis_index("cl") == lax.axis_index("tensor") % 2
    return jnp.where(stays, value, received)


def gather_weights(first, second):
    core = lax.axis_index("core")
    mine = jnp.where(core == 0, first, second)
    received = swapped(jnp.where(core == 0, second, first), "core", 1)
    rows, cols = mine.shape
    pair = jnp.stack(
        [jnp.where(core == 0, mine, received), jnp.where(core == 0, received, mine)]
    )
    pair = traded(pair.reshape(2 * rows, cols))
    full = lax.all_gather(pair, SPREAD, axis=0, tiled=True)
    lanes, px, groups = (lax.axis_size(axis) for axis in SPREAD)
    return full.reshape(lanes // 2, 2, px, groups, 2, rows, cols)


def whole_rows(gathered, first, width):
    pieces = [
        jnp.transpose(part[..., first : first + width], (1, 3, 2, 0, 4, 5)).reshape(-1, width)
        for part in gathered
    ]
    return jnp.concatenate(pieces, 1)


def split_rows(grad):
    px, groups = lax.axis_size("px"), lax.axis_size("cg")
    rows = grad.shape[0] // (4 * px * groups)
    shaped = grad.reshape(px, 2, groups, 2, rows, grad.shape[1])
    return jnp.transpose(shaped, (3, 0, 2, 1, 4, 5)).reshape(-1, grad.shape[1])


def joined_grads(by_k):
    return jnp.concatenate(
        [jnp.concatenate([split_rows(part) for part in parts], 1) for parts in by_k], 0
    )


def scatter_grads(joined):
    core = lax.axis_index("core")
    summed = traded(lax.psum_scatter(joined, SPREAD, scatter_dimension=0, tiled=True))
    rows = summed.shape[0] // 2
    top, bottom = summed[:rows], summed[rows:]
    mine = jnp.where(core == 0, top, bottom)
    received = swapped(jnp.where(core == 0, bottom, top), "core", 1)
    first = jnp.where(core == 0, mine, received).astype(jnp.float32)
    second = jnp.where(core == 0, received, mine).astype(jnp.float32)
    return first, second


def columns_of(array, groups):
    width = array.shape[1] // groups
    return [array[:, n * width : (n + 1) * width] for n in range(groups)]


def padded_cols(array, width):
    return jnp.pad(array, ((0, 0), (0, width - array.shape[1])))


def up_to(value, step):
    return -(-value // step) * step


def shards(
    tokens,
    seg_starts,
    norm_gain,
    w_query,
    w_key,
    w_value,
    w_gate,
    w_alpha,
    w_beta,
    conv_query,
    conv_key,
    conv_value,
    a_log,
    dt_bias,
    out_gain,
    w_out,
    ffn_gain,
    w_ffn_gate,
    w_ffn_up,
    w_ffn_down,
    d_mixed,
):
    low = jnp.bfloat16
    core = lax.axis_index("core")
    lane = lax.axis_index("tensor")
    side = lax.axis_index("cl")
    place = lax.axis_index("cg")
    lanes = lax.axis_size("tensor")
    pieces = lax.axis_size("cg")
    groups = lanes // 2
    model = tokens.shape[2]
    length = 2 * tokens.shape[1] * lanes
    own_seqs = tokens.shape[0] // lanes
    seqs = 2 * own_seqs
    flat = seqs * length
    quarter_heads = w_alpha.shape[1]
    per_quarter = quarter_heads // 2
    heads = per_quarter * groups
    units = w_ffn_gate.shape[1]
    half_units = units // 2
    wide = up_to(half_units, 128)
    val_cols = per_quarter * VAL
    count = length // CHUNK

    def head_block(number):
        key = slice(number * KEY, (number + 1) * KEY)
        val = slice(number * VAL, (number + 1) * VAL)
        one = slice(number, number + 1)
        parts = [w_query[:, key], w_key[:, key], w_value[:, val], w_gate[:, val]]
        return padded_cols(
            jnp.concatenate(parts + [w_alpha[:, one], w_beta[:, one]], 1), HEAD
        )

    def mix_half(half):
        numbers = range(half * per_quarter, (half + 1) * per_quarter)
        return jnp.concatenate([head_block(number) for number in numbers], 1)

    def rest_half(half):
        inner = slice(half * half_units, (half + 1) * half_units)
        outer = slice(half * val_cols, (half + 1) * val_cols)
        parts = [w_ffn_gate[:, inner], w_ffn_up[:, inner], w_ffn_down[inner].T]
        return jnp.concatenate(
            [padded_cols(part, wide) for part in parts] + [w_out[outer].T], 1
        )

    def of_heads(array, width):
        shaped = array.reshape(array.shape[0], groups, 2, 2, per_quarter * width)
        mine = jnp.where(side == 0, shaped[:, :, 0], shaped[:, :, 1])
        mine = jnp.where(core == 0, mine[:, :, 0], mine[:, :, 1])
        return mine.reshape(array.shape[0], heads, width)

    mix_parts = gather_weights(mix_half(0), mix_half(1))
    own = dealt_by_sequence(tokens).astype(jnp.float32)
    normed_own = (rms_rows(own) * norm_gain).astype(low)
    normed = with_group(normed_own).reshape(flat, model)
    rest_parts = gather_weights(rest_half(0), rest_half(1))
    w_mix = whole_rows(mix_parts, 0, per_quarter * HEAD)
    pre = matmul(normed, w_mix).reshape(seqs, length, heads * HEAD)
    rim = jnp.zeros((seqs, RIM, heads * HEAD), jnp.float32)
    if pieces > 1:
        rim = passed_along(pre[:, length - RIM :], "cg", 1)
    starts_own = lax.dynamic_slice_in_dim(seg_starts, lane * own_seqs, own_seqs, 0)
    starts = with_partner(starts_own.astype(jnp.float32)).astype(jnp.int32)
    base = place * length
    seg_ext = seg_ids(starts, base + jnp.arange(-3, length, dtype=jnp.int32))
    segs = jnp.stack(
        [seg_ext[:, 3 - n : 3 - n + length].reshape(seqs, count, CHUNK) for n in range(4)], 2
    ).astype(jnp.float32)
    segs = jnp.pad(segs, ((0, 0), (0, 0), (0, 4), (0, 0)))
    taps = jnp.concatenate(
        [of_heads(conv_query, KEY), of_heads(conv_key, KEY), of_heads(conv_value, VAL)], 2
    ).reshape(4, heads * GATE_AT)
    par = jnp.stack(
        [of_heads(-jnp.exp(a_log)[None], 1)[0, :, 0], of_heads(dt_bias[None], 1)[0, :, 0]], 1
    )
    par = jnp.broadcast_to(
        jnp.pad(par, ((0, 0), (0, 6)))[:, :, None], (heads, 8, 128)
    )
    gain_row = out_gain[None]
    front = (pre, rim, taps, par, segs)
    cot_own = dealt_by_sequence(d_mixed)
    cot = with_group(cot_own).reshape(flat, model)
    if pieces == 1:
        inverse, step, read, states, mixer, gated = run_whole(*front, gain_row)
    else:
        inverse, step, push, read, base_out, end_map, end_push = run_front(*front)
        state_in = passed_along(end_push, "cg", 1)
        state_in = lax.fori_loop(
            0,
            pieces - 2,
            lambda turn, state: passed_along(apply_map(end_map, state) + end_push, "cg", 1),
            state_in,
        )
        states, mixer, gated = run_output(state_in, step, push, read, base_out, pre, gain_row)
    gated_flat = gated.reshape(flat, heads * VAL)
    w_pair = jnp.concatenate(
        [whole_rows(rest_parts, 0, wide), whole_rows(rest_parts, wide, wide)], 1
    )
    w_down_t = whole_rows(rest_parts, 2 * wide, wide)
    w_out_t = whole_rows(rest_parts, 3 * wide, val_cols)
    attn_part = matmul_right_t(gated_flat, w_out_t).astype(low)
    middle = own + sum_in_group(attn_part.reshape(seqs, length, model))
    normed_two_own = (rms_rows(middle) * ffn_gain).astype(low)
    normed_two = with_group(normed_two_own).reshape(flat, model)
    width = groups * wide
    pair = matmul(normed_two, w_pair)
    gate_pre, up_pre = pair[:, :width], pair[:, width:]
    sigma = jax.nn.sigmoid(gate_pre)
    hidden = (gate_pre * sigma * up_pre).astype(low)
    d_hidden = matmul(cot, w_down_t)
    d_gate_pre = (d_hidden * up_pre * sigma * (1.0 + gate_pre * (1.0 - sigma))).astype(low)
    d_up_pre = (d_hidden * gate_pre * sigma).astype(low)
    d_pair = jnp.concatenate([d_gate_pre, d_up_pre], 1)
    ffn_terms = matmul_right_t(d_pair, w_pair).astype(low)
    d_normed_two = sum_in_group(ffn_terms.reshape(seqs, length, model))
    _, norm_two_back = jax.vjp(norm_scaled, middle, ffn_gain)
    d_middle_part, grad_ffn_gain = norm_two_back(d_normed_two)
    d_middle = cot_own.astype(jnp.float32) + d_middle_part
    grad_pair = matmul_left_t(normed_two, d_pair).astype(low)
    grad_down = matmul_left_t(cot, hidden).astype(low)
    rest_joined = joined_grads(
        zip(
            columns_of(grad_pair[:, :width], groups),
            columns_of(grad_pair[:, width:], groups),
            columns_of(grad_down, groups),
        )
    )
    d_branch = with_group(d_middle.astype(low)).reshape(flat, model)
    d_branch, rest_joined = lax.optimization_barrier((d_branch, rest_joined))
    rest_first, rest_second = scatter_grads(rest_joined)
    d_gated = matmul(d_branch, w_out_t).reshape(seqs, length, heads * VAL)
    if pieces == 1:
        ends = (read,)
    else:
        pull, d_start = run_pull(d_gated, mixer, pre, gain_row, step, read)
        d_end = passed_along(d_start, "cg", -1)
        d_end = lax.fori_loop(
            0,
            pieces - 2,
            lambda turn, state: passed_along(apply_map_t(end_map, state) + d_start, "cg", -1),
            d_end,
        )
        ends = (pull, d_end)
    ffn_part = matmul_right_t(hidden, w_down_t).astype(low)
    ffn_own = sum_in_group(ffn_part.reshape(seqs, length, model))
    mixed = dealt_by_tokens((middle + ffn_own).astype(low))
    d_all, d_rim, d_small = run_back(*front, inverse, step, states, d_gated, mixer, gain_row, *ends)
    if pieces > 1:
        back_rim = passed_along(d_rim, "cg", -1).reshape(seqs, RIM, heads, GATE_AT)
        back_rim = jnp.pad(back_rim, ((0, 0),) * 3 + ((0, HEAD - GATE_AT),))
        tail = d_all[:, length - RIM :].astype(jnp.float32) + back_rim.reshape(seqs, RIM, -1)
        d_all = lax.dynamic_update_slice(d_all, tail.astype(low), (0, length - RIM, 0))
    d_all = d_all.reshape(flat, heads * HEAD)
    grad_mix = matmul_left_t(normed, d_all).astype(low)
    grad_out = matmul_left_t(d_branch, gated_flat).astype(low)
    mix_joined = joined_grads(zip(columns_of(grad_mix, groups), columns_of(grad_out, groups)))
    mix_first, mix_second = scatter_grads(mix_joined)
    d_normed = matmul_right_t(d_all, w_mix).astype(low)
    own_d_normed = sum_in_group(d_normed.reshape(seqs, length, model))
    _, norm_back = jax.vjp(norm_scaled, own, norm_gain)
    d_own, grad_norm_gain = norm_back(own_d_normed)
    grad_tokens = dealt_by_tokens((d_middle + d_own).astype(low)).astype(jnp.float32)

    small = jnp.sum(d_small, axis=0)

    def placed(part):
        rows, _, each = part.shape
        shaped = part.reshape(rows, groups, 1, 1, per_quarter * each)
        spots = jnp.arange(4).reshape(1, 1, 2, 2, 1)
        return jnp.where(spots == 2 * side + core, shaped, 0.0).reshape(-1)

    conv_parts = jnp.transpose(small[:, :4], (1, 0, 2))
    items = [
        grad_ffn_gain,
        placed(conv_parts[..., :KEY]),
        placed(conv_parts[..., KEY : 2 * KEY]),
        placed(conv_parts[..., 2 * KEY :]),
        jnp.sum(small[:, 4, :VAL], axis=0),
        placed(small[None, :, 5, :1]),
        placed(small[None, :, 6, :1]),
    ]
    sizes = [item.shape[0] for item in items]
    total = up_to(sum(sizes), 1024)
    joined = jnp.concatenate(items + [jnp.zeros((total - sum(sizes),), jnp.float32)])
    joined = summed_everywhere(joined.reshape(-1, 128)).reshape(-1)
    norm_sum = summed_everywhere(grad_norm_gain.reshape(8, -1)).reshape(-1)
    ends = [sum(sizes[: n + 1]) for n in range(len(sizes))]
    sums = [joined[end - size : end] for size, end in zip(sizes, ends)]

    def mix_cols(first, width):
        halves_of = [
            half[:, : per_quarter * HEAD].reshape(half.shape[0], per_quarter, HEAD)[:, :, first : first + width].reshape(
                half.shape[0], -1
            )
            for half in (mix_first, mix_second)
        ]
        return jnp.concatenate(halves_of, 1)

    def rest_cols(first, width, pair=(rest_first, rest_second)):
        return jnp.concatenate([half[:, first : first + width] for half in pair], 1)

    return (
        mixed,
        grad_tokens,
        norm_sum,
        mix_cols(0, KEY),
        mix_cols(KEY, KEY),
        mix_cols(2 * KEY, VAL),
        mix_cols(GATE_AT, VAL),
        mix_cols(AB_AT, 1),
        mix_cols(AB_AT + 1, 1),
        sums[1].reshape(4, -1),
        sums[2].reshape(4, -1),
        sums[3].reshape(4, -1),
        sums[5],
        sums[6],
        sums[4],
        rest_cols(per_quarter * HEAD, val_cols, (mix_first, mix_second)).T,
        sums[0],
        rest_cols(0, half_units),
        rest_cols(wide, half_units),
        rest_cols(2 * wide, half_units).T,
    )


def solution(mesh):
    sizes = tuple(mesh.shape[axis] for axis in ("dp", "ctx", "tensor"))
    fine = Mesh(
        mesh.devices.reshape(sizes[0] // 2, 2, sizes[1] // 2, 2, sizes[2]),
        ("px", "core", "cg", "cl", "tensor"),
    )
    dp = ("px", "core")
    rows = P(("px", "core", "cg", "cl"), "tensor")
    cols = P("tensor", ("px", "core", "cg", "cl"))
    own = P(dp, ("cg", "cl", "tensor"), None)
    return jax.shard_map(
        shards,
        mesh=fine,
        in_specs=(own, P(dp, None), P())
        + (rows,) * 6
        + (P(),) * 6
        + (cols, P(), rows, rows, cols, own),
        out_specs=(own, own, P())
        + (rows,) * 6
        + (P(),) * 6
        + (cols, P(), rows, rows, cols),
        check_vma=False,
    )
```

```python
from functools import partial

import jax
import jax.numpy as jnp
from jax import lax
from jax.experimental import pallas as pl
from jax.experimental.pallas import tpu as pltpu
from jax.sharding import Mesh, PartitionSpec as P

CHUNK = 128
RIM = 8
EPS_NORM = 1e-05
EPS_UNIT = 1e-06
FULL_ACCURACY = lax.Precision.HIGHEST
NN = (((1,), (0,)), ((), ()))
NT = (((1,), (1,)), ((), ()))
TN = (((0,), (0,)), ((), ()))


def dot_low(left, right, dims):
    return lax.dot_general(
        left.astype(jnp.bfloat16),
        right.astype(jnp.bfloat16),
        dims,
        preferred_element_type=jnp.float32,
    )


def halves(value):
    high = value.astype(jnp.bfloat16)
    return high, (value - high.astype(jnp.float32)).astype(jnp.bfloat16)


def dot_split(left, right, dims):
    left_high, left_low = halves(left)
    right_high, right_low = halves(right)
    total = lax.dot_general(left_high, right_high, dims, preferred_element_type=jnp.float32)
    total += lax.dot_general(left_high, right_low, dims, preferred_element_type=jnp.float32)
    return total + lax.dot_general(left_low, right_high, dims, preferred_element_type=jnp.float32)


def sigmoid(value):
    return 1.0 / (1.0 + jnp.exp(-value))


def positions():
    row = lax.broadcasted_iota(jnp.int32, (CHUNK, CHUNK), 0)
    col = lax.broadcasted_iota(jnp.int32, (CHUNK, CHUNK), 1)
    return row, col


def unit_lower_inverses(lowers):
    row, col = positions()
    eye = (row == col).astype(jnp.float32)
    diag = [jnp.where(row // 8 == col // 8, low, 0.0) for low in lowers]
    result = [eye - d for d in diag]
    power = [dot_split(d, d, NN) for d in diag]
    result = [x + dot_split(x, p, NN) for x, p in zip(result, power)]
    power = [dot_split(p, p, NN) for p in power]
    result = [x + dot_split(x, p, NN) for x, p in zip(result, power)]
    size = 8
    while size < CHUNK:
        across = (row // (2 * size) == col // (2 * size)) & (row // size != col // size)
        mixed = [dot_split(jnp.where(across, low, 0.0), x, NN) for low, x in zip(lowers, result)]
        result = [x - dot_split(x, m, NN) for x, m in zip(result, mixed)]
        size *= 2
    return result


KEY = 128
VAL = 256
GATE_AT = 2 * KEY + VAL
AB_AT = GATE_AT + VAL
HEAD = AB_AT + 128
VMEM_BYTES = 48 * 2**20


def thirds(value):
    high = value.astype(jnp.bfloat16)
    rest = value - high.astype(jnp.float32)
    middle = rest.astype(jnp.bfloat16)
    return high, middle, (rest - middle.astype(jnp.float32)).astype(jnp.bfloat16)


def dot_ones(ones, value, dims):
    left = ones.astype(jnp.bfloat16)
    return sum(
        lax.dot_general(left, part, dims, preferred_element_type=jnp.float32)
        for part in thirds(value)
    )


def unit(values):
    scale = lax.rsqrt(jnp.sum(values * values, axis=-1, keepdims=True) + EPS_UNIT)
    return values * scale, scale


def last_value(column):
    return column[CHUNK - 1 : CHUNK, :]


def spread_lanes(column):
    return jnp.broadcast_to(column, (CHUNK, CHUNK))


def chunk_parts(pre, par, segs, index):
    rows = slice(index * CHUNK, (index + 1) * CHUNK)
    row, col = positions()
    tile = segs[0, index]
    columns = jnp.concatenate([tile, jnp.zeros((CHUNK - 8, CHUNK), jnp.float32)], axis=0).T
    seg = columns[:, 0:1]
    masks = [(seg == columns[:, n : n + 1]).astype(jnp.float32) for n in range(1, 4)]
    shifted = pre[0, rows, AB_AT : AB_AT + 1] + par[0, 1:2, 0:1]
    strength = sigmoid(pre[0, rows, AB_AT + 1 : AB_AT + 2])
    soft = jnp.maximum(shifted, 0.0) + jnp.log1p(jnp.exp(-jnp.abs(shifted)))
    decay = par[0, 0:1, 0:1] * soft
    lower = (row >= col).astype(jnp.float32)
    cumul = dot_ones(lower, spread_lanes(decay), NN)
    allowed = (row >= col) & (seg == tile[0:1, :])
    within = jnp.where(allowed, jnp.exp(jnp.minimum(cumul - cumul.T, 0.0)), 0.0)
    cum = cumul[:, 0:1]
    opening = jnp.where(seg == tile[1:2, 0:1], jnp.exp(cum), 0.0)
    closing = jnp.where(
        seg == tile[0:1, CHUNK - 1 :], jnp.exp(jnp.minimum(last_value(cum) - cum, 0.0)), 0.0
    )
    return dict(
        rows=rows,
        masks=masks,
        shifted=shifted,
        decay=decay,
        strength=strength,
        opening=opening,
        closing=closing,
        within=within,
    )


def fill_ext(ext, rim, pre):
    ext[0:RIM, :] = rim[0, :, :GATE_AT]
    ext[RIM:, :] = pre[0, :, :GATE_AT]


def conv_chunk(ext, taps, part):
    first = RIM + part["rows"].start
    total = taps[0:1, :] * ext[first : first + CHUNK, :]
    for offset in range(1, 4):
        shifted = ext[first - offset : first - offset + CHUNK, :]
        total = total + taps[offset : offset + 1, :] * shifted * part["masks"][offset - 1]
    return total


def split_qkv(array):
    return array[:, :KEY], array[:, KEY : 2 * KEY], array[:, 2 * KEY :]

GROUP = 4


def front_terms(pre, ext, taps, par, segs, first, last):
    row, col = positions()
    eye = (row == col).astype(jnp.float32)
    parts = [chunk_parts(pre, par, segs, n) for n in range(first, last)]
    convs = [conv_chunk(ext, taps, p) for p in parts]
    acts = [split_qkv(c * sigmoid(c)) for c in convs]
    queries = [unit(a[0])[0] * (float(KEY) ** -0.5) for a in acts]
    keys = [unit(a[1])[0] for a in acts]
    inner = [dot_split(k, k, NT) for k in keys]
    lowers = [
        jnp.where(row > col, p["strength"] * p["within"] * i, 0.0) for p, i in zip(parts, inner)
    ]
    inverses = unit_lower_inverses(lowers)
    scores = [dot_low(q, k, NT) * p["within"] for q, k, p in zip(queries, keys, parts)]
    known = [
        dot_low(t, p["strength"] * a[2], NN) for t, p, a in zip(inverses, parts, acts)
    ]
    write = [
        dot_low(t, p["strength"] * p["opening"] * k, NN)
        for t, p, k in zip(inverses, parts, keys)
    ]
    closed = [p["closing"] * k for p, k in zip(parts, keys)]
    steps = [
        last_value(p["opening"]) * eye - dot_low(c, w, TN)
        for p, c, w in zip(parts, closed, write)
    ]
    pushes = [dot_low(c, u, TN) for c, u in zip(closed, known)]
    reads = [
        p["opening"] * q - dot_low(s, w, NN)
        for p, q, s, w in zip(parts, queries, scores, write)
    ]
    bases = [dot_low(s, u, NN) for s, u in zip(scores, known)]
    return inverses, steps, pushes, reads, bases


def write_output(state, base, read, pre, gain, rows, mixer_out, gated_out):
    mixer = base + dot_low(read, state, NN)
    mixer_out[0, 0, rows, :] = mixer
    scale = lax.rsqrt(jnp.mean(mixer * mixer, axis=-1, keepdims=True) + EPS_NORM)
    gate = pre[0, rows, GATE_AT:AB_AT]
    gated_out[0, rows, :] = (mixer * scale * gain[...] * gate * sigmoid(gate)).astype(
        jnp.bfloat16
    )


def chunk_rows(number):
    return slice(number * CHUNK, (number + 1) * CHUNK)


def front_kernel(
    pre, rim, taps, par, segs,
    inverse_out, step_out, push_out, read_out, base_out, end_map, end_push,
    ext,
):
    count = pre.shape[1] // CHUNK
    fill_ext(ext, rim, pre)
    total_map = total_push = None
    for first in range(0, count, GROUP):
        last = min(count, first + GROUP)
        terms = front_terms(pre, ext, taps, par, segs, first, last)
        for n in range(first, last):
            rows = chunk_rows(n)
            inverse, step, push, read, base = (term[n - first] for term in terms)
            inverse_out[0, 0, rows, :] = inverse
            step_out[0, 0, rows, :] = step
            push_out[0, 0, rows, :] = push
            read_out[0, 0, rows, :] = read
            base_out[0, 0, rows, :] = base
            if n:
                total_push = dot_low(step, total_push, NN) + push
                total_map = dot_low(step, total_map, NN)
            else:
                total_map, total_push = step, push
    end_map[0, 0] = total_map
    end_push[0, 0] = total_push


def whole_kernel(
    pre, rim, taps, par, segs, gain,
    inverse_out, step_out, read_out, states_out, mixer_out, gated_out,
    ext,
):
    count = pre.shape[1] // CHUNK
    fill_ext(ext, rim, pre)
    state = jnp.zeros((KEY, VAL), jnp.float32)
    for first in range(0, count, GROUP):
        last = min(count, first + GROUP)
        terms = front_terms(pre, ext, taps, par, segs, first, last)
        for n in range(first, last):
            rows = chunk_rows(n)
            inverse, step, push, read, base = (term[n - first] for term in terms)
            inverse_out[0, 0, rows, :] = inverse
            step_out[0, 0, rows, :] = step
            read_out[0, 0, rows, :] = read
            states_out[0, 0, rows, :] = state
            write_output(state, base, read, pre, gain, rows, mixer_out, gated_out)
            state = dot_low(step, state, NN) + push


def output_kernel(
    state_in, step, push, read, base, pre, gain, states_out, mixer_out, gated_out
):
    count = step.shape[2] // CHUNK
    state = state_in[0, 0]
    for n in range(count):
        rows = chunk_rows(n)
        states_out[0, 0, rows, :] = state
        write_output(
            state, base[0, 0, rows, :], read[0, 0, rows, :], pre, gain, rows, mixer_out, gated_out
        )
        if n < count - 1:
            state = dot_low(step[0, 0, rows, :], state, NN) + push[0, 0, rows, :]


def mixer_back(d_gated, mixer_in, pre, gain, rows):
    mixer = mixer_in[0, 0, rows, :]
    scale = lax.rsqrt(jnp.mean(mixer * mixer, axis=-1, keepdims=True) + EPS_NORM)
    normed = mixer * scale
    gate = pre[0, rows, GATE_AT:AB_AT]
    sig = sigmoid(gate)
    grad = d_gated[0, rows, :]
    through = grad * gate * sig
    d_normed = through * gain[...]
    d_mixer = scale * (d_normed - normed * jnp.mean(d_normed * normed, axis=-1, keepdims=True))
    d_gate = grad * normed * gain[...] * sig * (1.0 + gate * (1.0 - sig))
    return d_mixer, d_gate, jnp.sum(through * normed, axis=0, keepdims=True)


def pull_kernel(d_gated, mixer_in, pre, gain, step, read, pull_out, start_out):
    count = step.shape[2] // CHUNK
    carried = None
    for n in reversed(range(count)):
        rows = slice(n * CHUNK, (n + 1) * CHUNK)
        d_mixer = mixer_back(d_gated, mixer_in, pre, gain, rows)[0]
        pull = dot_low(read[0, 0, rows, :], d_mixer, TN)
        pull_out[0, 0, rows, :] = pull
        if carried is None:
            carried = pull
        else:
            carried = dot_low(step[0, 0, rows, :], carried, TN) + pull
    start_out[0, 0] = carried


def back_kernel(alone, pre, rim, taps, par, segs, inverse, step, states, d_gated, mixer_in, gain, *refs):
    if alone:
        read, d_all_out, d_rim_out, d_small_out, ext, pad = refs
    else:
        pull, d_end, d_all_out, d_rim_out, d_small_out, ext, pad = refs
    length = pre.shape[1]
    count = length // CHUNK
    fill_ext(ext, rim, pre)
    row, col = positions()
    lane = col
    last_row = lax.broadcasted_iota(jnp.int32, (CHUNK, 1), 0) == CHUNK - 1
    lower = (row >= col).astype(jnp.float32)
    d_states = [None] * count
    d_states[count - 1] = jnp.zeros((KEY, VAL), jnp.float32) if alone else d_end[0, 0]
    for n in reversed(range(1, count)):
        block = chunk_rows(n)
        if alone:
            d_mixer = mixer_back(d_gated, mixer_in, pre, gain, block)[0]
            back = dot_low(read[0, 0, block, :], d_mixer, TN)
        else:
            back = pull[0, 0, block, :]
        d_states[n - 1] = dot_low(step[0, 0, block, :], d_states[n], TN) + back
    pad[:, 0:RIM, :] = jnp.zeros((4, RIM, GATE_AT), jnp.float32)
    pad[:, RIM + length :, :] = jnp.zeros((4, RIM, GATE_AT), jnp.float32)
    d_gain = jnp.zeros((1, VAL), jnp.float32)
    d_log = jnp.zeros((1, 1), jnp.float32)
    d_bias = jnp.zeros((1, 1), jnp.float32)
    d_taps = [jnp.zeros((1, GATE_AT), jnp.float32) for _ in range(4)]
    for n in range(count):
        part = chunk_parts(pre, par, segs, n)
        block, within = part["rows"], part["within"]
        strength, opening, closing = part["strength"], part["opening"], part["closing"]
        conv = conv_chunk(ext, taps, part)
        sig = sigmoid(conv)
        act_q, act_k, value = split_qkv(conv * sig)
        unit_q, scale_q = unit(act_q)
        key, scale_k = unit(act_k)
        query = unit_q * (float(KEY) ** -0.5)
        state, d_state = states[0, 0, block, :], d_states[n]
        solve = inverse[0, 0, block, :]
        grad, d_gate, d_gain_part = mixer_back(d_gated, mixer_in, pre, gain, block)
        d_gain = d_gain + d_gain_part
        rest = value - opening * dot_low(key, state, NN)
        update = dot_low(solve, strength * rest, NN)
        scores = dot_low(query, key, NT) * within
        inner = dot_low(key, key, NT) * within
        closed = closing * key
        d_update = dot_low(scores, grad, TN) + dot_low(closed, d_state, NN)
        d_right = dot_low(solve, d_update, TN)
        d_scores = dot_low(grad, update, NT)
        d_lower = jnp.where(row > col, -dot_low(d_right, update, NT), 0.0)
        d_plain = d_scores * within
        d_inner = d_lower * strength * within
        read_back = dot_low(grad, state, NT)
        known_back = -dot_low(strength * d_right, state, NT)
        closed_back = dot_low(update, d_state, NT)
        d_query = opening * read_back + dot_low(d_plain, key, NN)
        d_key = (
            dot_low(d_plain, query, TN)
            + dot_low(d_inner, key, NN)
            + dot_low(d_inner, key, TN)
            + opening * known_back
            + closing * closed_back
        )
        lower_parts = d_lower * inner
        d_strength = jnp.sum(lower_parts, axis=1, keepdims=True) + jnp.sum(
            d_right * rest, axis=1, keepdims=True
        )
        spread = d_scores * scores + strength * lower_parts
        d_opening = jnp.sum(query * read_back + key * known_back, axis=1, keepdims=True)
        d_closing = jnp.sum(key * closed_back, axis=1, keepdims=True) * closing
        through = jnp.sum(
            jnp.sum(state * d_state, axis=1, keepdims=True), axis=0, keepdims=True
        )
        end_sum = jnp.sum(d_closing, axis=0, keepdims=True) + through * last_value(opening)
        d_cumul = (
            jnp.sum(spread, axis=1, keepdims=True)
            + d_opening * opening
            - d_closing
            + jnp.where(last_row, end_sum, 0.0)
        )
        down = spread_lanes(jnp.sum(spread, axis=0, keepdims=True)).T
        d_decay = dot_ones(lower, spread_lanes(d_cumul) - down, TN)[:, 0:1]
        d_alpha = d_decay * par[0, 0:1, 0:1] * sigmoid(part["shifted"])
        d_beta = d_strength * strength * (1.0 - strength)
        d_log = d_log + jnp.sum(d_decay * part["decay"], axis=0, keepdims=True)
        d_bias = d_bias + jnp.sum(d_alpha, axis=0, keepdims=True)
        d_all_out[0, block, GATE_AT:AB_AT] = d_gate.astype(jnp.bfloat16)
        d_all_out[0, block, AB_AT:] = jnp.where(
            lane == 0, d_alpha, jnp.where(lane == 1, d_beta, 0.0)
        ).astype(jnp.bfloat16)
        d_query = d_query * (float(KEY) ** -0.5)
        d_act = jnp.concatenate(
            [
                scale_q * (d_query - unit_q * jnp.sum(unit_q * d_query, axis=-1, keepdims=True)),
                scale_k * (d_key - key * jnp.sum(key * d_key, axis=-1, keepdims=True)),
                strength * d_right,
            ],
            axis=1,
        )
        d_conv = d_act * sig * (1.0 + conv * (1.0 - sig))
        first = RIM + block.start
        for offset in range(4):
            masked = d_conv if offset == 0 else d_conv * part["masks"][offset - 1]
            shifted = ext[first - offset : first - offset + CHUNK, :]
            d_taps[offset] = d_taps[offset] + jnp.sum(masked * shifted, axis=0, keepdims=True)
            pad[offset, first : first + CHUNK, :] = masked * taps[offset : offset + 1, :]
    d_rim = pad[0, 0:RIM, :]
    for offset in range(1, 4):
        d_rim = d_rim + pad[offset, offset : offset + RIM, :]
    d_rim_out[0] = d_rim
    for n in range(count):
        first = RIM + n * CHUNK
        total = pad[0, first : first + CHUNK, :]
        for offset in range(1, 4):
            total = total + pad[offset, first + offset : first + offset + CHUNK, :]
        d_all_out[0, n * CHUNK : (n + 1) * CHUNK, :GATE_AT] = total.astype(jnp.bfloat16)
    for offset in range(4):
        d_small_out[0, 0, offset : offset + 1, :] = d_taps[offset]
    d_small_out[0, 0, 4:5, :] = jnp.concatenate([d_gain, d_gain], axis=1)
    d_small_out[0, 0, 5:6, :] = jnp.broadcast_to(d_log, (1, GATE_AT))
    d_small_out[0, 0, 6:7, :] = jnp.broadcast_to(d_bias, (1, GATE_AT))
    d_small_out[0, 0, 7:8, :] = jnp.zeros((1, GATE_AT), jnp.float32)


def per_head(*tail):
    return pl.BlockSpec((1, 1) + tail, lambda s, h: (s, h) + (0,) * len(tail))


def lanes_at(rows, width):
    return pl.BlockSpec((1, rows, width), lambda s, h: (s, 0, h))


def front_specs(length):
    return [
        lanes_at(length, HEAD),
        lanes_at(RIM, HEAD),
        pl.BlockSpec((4, GATE_AT), lambda s, h: (0, h)),
        pl.BlockSpec((1, 8, 128), lambda s, h: (h, 0, 0)),
        pl.BlockSpec((1, length // CHUNK, 8, CHUNK), lambda s, h: (s, 0, 0, 0)),
    ]


def gain_spec():
    return pl.BlockSpec((1, VAL), lambda s, h: (0, 0))


def shape(dims, kind=jnp.float32):
    return jax.ShapeDtypeStruct(dims, kind)


def call(kernel, lead, in_specs, outs, scratch, units, args):
    length = args[0].shape[1] if args[0].ndim == 3 else args[1].shape[2]
    flops = lead[0] * lead[1] * length * 128 * 128 * 2 * units
    return pl.pallas_call(
        kernel,
        grid=lead,
        in_specs=in_specs,
        out_specs=[spec for spec, _ in outs],
        out_shape=[kind for _, kind in outs],
        scratch_shapes=[pltpu.VMEM(dims, jnp.float32) for dims in scratch],
        compiler_params=pltpu.CompilerParams(vmem_limit_bytes=VMEM_BYTES),
        cost_estimate=pl.CostEstimate(
            flops=flops, bytes_accessed=flops // 100, transcendentals=0
        ),
    )(*args)


def run_front(pre, rim, taps, par, segs):
    seqs, length, wide = pre.shape
    lead = (seqs, wide // HEAD)
    widths = (KEY, KEY, VAL, KEY, VAL)
    outs = [(per_head(length, width), shape(lead + (length, width))) for width in widths]
    outs += [(per_head(KEY, width), shape(lead + (KEY, width))) for width in (KEY, VAL)]
    return call(
        front_kernel,
        lead,
        front_specs(length),
        outs,
        [(length + RIM, GATE_AT)],
        60,
        (pre, rim, taps, par, segs),
    )


def run_output(state_in, step, push, read, base, pre, gain):
    seqs, heads, length, _ = step.shape
    lead = (seqs, heads)
    in_specs = [per_head(KEY, VAL)]
    in_specs += [per_head(length, width) for width in (KEY, VAL, KEY, VAL)]
    in_specs += [lanes_at(length, HEAD), gain_spec()]
    outs = [
        (per_head(length, VAL), shape(lead + (length, VAL))),
        (per_head(length, VAL), shape(lead + (length, VAL))),
        (lanes_at(length, VAL), shape((seqs, length, heads * VAL), jnp.bfloat16)),
    ]
    args = (state_in, step, push, read, base, pre, gain)
    return call(output_kernel, lead, in_specs, outs, [], 15, args)


def run_pull(d_gated, mixer, pre, gain, step, read):
    seqs, heads, length, _ = step.shape
    lead = (seqs, heads)
    in_specs = [lanes_at(length, VAL), per_head(length, VAL), lanes_at(length, HEAD)]
    in_specs += [gain_spec(), per_head(length, KEY), per_head(length, KEY)]
    outs = [
        (per_head(length, VAL), shape(lead + (length, VAL))),
        (per_head(KEY, VAL), shape(lead + (KEY, VAL))),
    ]
    return call(
        pull_kernel, lead, in_specs, outs, [], 15, (d_gated, mixer, pre, gain, step, read)
    )


def run_whole(pre, rim, taps, par, segs, gain):
    seqs, length, wide = pre.shape
    heads = wide // HEAD
    lead = (seqs, heads)
    widths = (KEY, KEY, KEY, VAL, VAL)
    outs = [(per_head(length, width), shape(lead + (length, width))) for width in widths]
    outs.append((lanes_at(length, VAL), shape((seqs, length, heads * VAL), jnp.bfloat16)))
    return call(
        whole_kernel,
        lead,
        front_specs(length) + [gain_spec()],
        outs,
        [(length + RIM, GATE_AT)],
        70,
        (pre, rim, taps, par, segs, gain),
    )


def run_back(pre, rim, taps, par, segs, inverse, step, states, d_gated, mixer, gain, *ends):
    seqs, length, wide = pre.shape
    heads = wide // HEAD
    lead = (seqs, heads)
    alone = len(ends) == 1
    in_specs = front_specs(length)
    in_specs += [per_head(length, width) for width in (KEY, KEY, VAL)]
    in_specs += [lanes_at(length, VAL), per_head(length, VAL), gain_spec()]
    in_specs += [per_head(length, KEY)] if alone else [per_head(length, VAL), per_head(KEY, VAL)]
    outs = [
        (lanes_at(length, HEAD), shape((seqs, length, wide), jnp.bfloat16)),
        (lanes_at(RIM, GATE_AT), shape((seqs, RIM, heads * GATE_AT))),
        (per_head(8, GATE_AT), shape(lead + (8, GATE_AT))),
    ]
    scratch = [(length + RIM, GATE_AT), (4, length + 2 * RIM, GATE_AT)]
    args = (pre, rim, taps, par, segs, inverse, step, states)
    args += (d_gated, mixer, gain) + ends
    return call(partial(back_kernel, alone), lead, in_specs, outs, scratch, 60, args)


def passed_along(value, axis, steps):
    count = lax.axis_size(axis)
    first, last = (max(0, -steps), min(count, count - steps))
    return lax.ppermute(value, axis, [(source, source + steps) for source in range(first, last)])


def swapped(value, axis, bits):
    count = lax.axis_size(axis)
    return lax.ppermute(value, axis, [(place, place ^ bits) for place in range(count)])


def summed_everywhere(value):
    for axis in ("core", "px", "cg", "cl", "tensor"):
        bits = 1
        while bits < lax.axis_size(axis):
            value = value + swapped(value, axis, bits)
            bits *= 2
    return value


def seg_ids(starts, spots):
    return jnp.sum((starts[:, None, :] <= spots[None, :, None]).astype(jnp.int32), axis=2) - 1


def rms_rows(values):
    return values * lax.rsqrt(jnp.mean(values * values, axis=-1, keepdims=True) + EPS_NORM)


def norm_scaled(values, gain):
    return rms_rows(values) * gain


def matmul(left, right):
    return lax.dot_general(left, right, NN, preferred_element_type=jnp.float32)


def matmul_left_t(left, right):
    return lax.dot_general(left, right, TN, preferred_element_type=jnp.float32)


def matmul_right_t(left, right):
    return lax.dot_general(left, right, NT, preferred_element_type=jnp.float32)


def apply_map(linear, state):
    return jnp.einsum("shij,shjv->shiv", linear, state, precision=FULL_ACCURACY)


def apply_map_t(linear, state):
    return jnp.einsum("shji,shjv->shiv", linear, state, precision=FULL_ACCURACY)


def dealt_by_sequence(own):
    lane, lanes = lax.axis_index("tensor"), lax.axis_size("tensor")
    each = own.shape[0] // lanes
    tokens = own.shape[1]
    result = jnp.zeros((each, tokens * lanes) + own.shape[2:], own.dtype)
    for bits in range(lanes):
        other = lane ^ bits
        part = lax.dynamic_slice_in_dim(own, other * each, each, 0)
        if bits:
            part = swapped(part, "tensor", bits)
        result = lax.dynamic_update_slice_in_dim(result, part, other * tokens, 1)
    return result


def dealt_by_tokens(rows):
    lane, lanes = lax.axis_index("tensor"), lax.axis_size("tensor")
    each, tokens = rows.shape[0], rows.shape[1] // lanes
    result = jnp.zeros((each * lanes, tokens) + rows.shape[2:], rows.dtype)
    for bits in range(lanes):
        other = lane ^ bits
        part = lax.dynamic_slice_in_dim(rows, other * tokens, tokens, 1)
        if bits:
            part = swapped(part, "tensor", bits)
        result = lax.dynamic_update_slice_in_dim(result, part, other * each, 0)
    return result


def with_partner(own):
    return jnp.concatenate([own, swapped(own, "core", 1)], 0)


def with_group(own):
    side = lax.axis_index("cl")
    tokens = own.shape[1]
    both = jnp.zeros((own.shape[0], 2 * tokens) + own.shape[2:], own.dtype)
    both = lax.dynamic_update_slice_in_dim(both, own, side * tokens, 1)
    both = lax.dynamic_update_slice_in_dim(
        both, swapped(own, "cl", 1), (1 - side) * tokens, 1
    )
    return with_partner(both)


def sum_of_cores(partial_sums):
    half = partial_sums.shape[0] // 2
    received = swapped(partial_sums[half:], "core", 1)
    both = partial_sums[:half].astype(jnp.float32) + received.astype(jnp.float32)
    return both.astype(partial_sums.dtype)


def sum_of_sides(both):
    side = lax.axis_index("cl")
    tokens = both.shape[1] // 2
    mine = lax.dynamic_slice_in_dim(both, side * tokens, tokens, 1)
    other = lax.dynamic_slice_in_dim(both, (1 - side) * tokens, tokens, 1)
    return mine.astype(jnp.float32) + swapped(other, "cl", 1).astype(jnp.float32)


def sum_in_group(partial_sums):
    return sum_of_sides(sum_of_cores(partial_sums))


SPREAD = ("tensor", "px", "cg")


def traded(value):
    lanes = lax.axis_size("tensor")
    pairs = [
        (side * lanes + lane, (1 - side) * lanes + (lane ^ 1))
        for side in range(2)
        for lane in range(lanes)
        if lane % 2 != side
    ]
    received = lax.ppermute(value, ("cl", "tensor"), pairs)
    stays = lax.axis_index("cl") == lax.axis_index("tensor") % 2
    return jnp.where(stays, value, received)


def gather_weights(first, second):
    core = lax.axis_index("core")
    mine = jnp.where(core == 0, first, second)
    received = swapped(jnp.where(core == 0, second, first), "core", 1)
    rows, cols = mine.shape
    pair = jnp.stack(
        [jnp.where(core == 0, mine, received), jnp.where(core == 0, received, mine)]
    )
    pair = traded(pair.reshape(2 * rows, cols))
    full = lax.all_gather(pair, SPREAD, axis=0, tiled=True)
    lanes, px, groups = (lax.axis_size(axis) for axis in SPREAD)
    return full.reshape(lanes // 2, 4 * px * groups * rows, cols)


def whole_rows(gathered, first, width):
    return jnp.concatenate([part[:, first : first + width] for part in gathered], 1)


def block_order():
    px, groups = lax.axis_size("px"), lax.axis_size("cg")
    return [
        ((place * 2 + core) * groups + group) * 2 + side
        for side in range(2)
        for place in range(px)
        for group in range(groups)
        for core in range(2)
    ]


def reordered(array, order):
    width = array.shape[-1] // len(order)
    return jnp.concatenate([array[..., n * width : (n + 1) * width] for n in order], -1)


def to_gather_order(array):
    return reordered(array, block_order())


def to_model_order(array):
    order = block_order()
    return reordered(array, [order.index(n) for n in range(len(order))])


def joined_grads(by_k):
    by_k = [list(parts) for parts in by_k]
    rows = by_k[0][0].shape[0]
    widths = [part.shape[1] for part in by_k[0]]
    joined = jnp.zeros((rows * len(by_k), sum(widths)), by_k[0][0].dtype)
    for n, parts in enumerate(by_k):
        for place, part in enumerate(parts):
            joined = lax.dynamic_update_slice(joined, part, (n * rows, sum(widths[:place])))
    return joined


def scatter_grads(joined):
    core = lax.axis_index("core")
    summed = traded(lax.psum_scatter(joined, SPREAD, scatter_dimension=0, tiled=True))
    rows = summed.shape[0] // 2
    top, bottom = summed[:rows], summed[rows:]
    mine = jnp.where(core == 0, top, bottom)
    received = swapped(jnp.where(core == 0, bottom, top), "core", 1)
    first = jnp.where(core == 0, mine, received).astype(jnp.float32)
    second = jnp.where(core == 0, received, mine).astype(jnp.float32)
    return first, second


def columns_of(array, groups):
    width = array.shape[1] // groups
    return [array[:, n * width : (n + 1) * width] for n in range(groups)]


def padded_cols(array, width):
    return jnp.pad(array, ((0, 0), (0, width - array.shape[1])))


def up_to(value, step):
    return -(-value // step) * step


def shards(
    tokens,
    seg_starts,
    norm_gain,
    w_query,
    w_key,
    w_value,
    w_gate,
    w_alpha,
    w_beta,
    conv_query,
    conv_key,
    conv_value,
    a_log,
    dt_bias,
    out_gain,
    w_out,
    ffn_gain,
    w_ffn_gate,
    w_ffn_up,
    w_ffn_down,
    d_mixed,
):
    low = jnp.bfloat16
    core = lax.axis_index("core")
    lane = lax.axis_index("tensor")
    side = lax.axis_index("cl")
    place = lax.axis_index("cg")
    lanes = lax.axis_size("tensor")
    pieces = lax.axis_size("cg")
    groups = lanes // 2
    model = tokens.shape[2]
    length = 2 * tokens.shape[1] * lanes
    own_seqs = tokens.shape[0] // lanes
    seqs = 2 * own_seqs
    flat = seqs * length
    quarter_heads = w_alpha.shape[1]
    per_quarter = quarter_heads // 2
    heads = per_quarter * groups
    units = w_ffn_gate.shape[1]
    half_units = units // 2
    wide = up_to(half_units, 128)
    val_cols = per_quarter * VAL
    count = length // CHUNK

    def head_block(number):
        key = slice(number * KEY, (number + 1) * KEY)
        val = slice(number * VAL, (number + 1) * VAL)
        one = slice(number, number + 1)
        parts = [w_query[:, key], w_key[:, key], w_value[:, val], w_gate[:, val]]
        return padded_cols(
            jnp.concatenate(parts + [w_alpha[:, one], w_beta[:, one]], 1), HEAD
        )

    def mix_half(half):
        numbers = range(half * per_quarter, (half + 1) * per_quarter)
        return jnp.concatenate([head_block(number) for number in numbers], 1)

    def rest_half(half):
        inner = slice(half * half_units, (half + 1) * half_units)
        outer = slice(half * val_cols, (half + 1) * val_cols)
        parts = [w_ffn_gate[:, inner], w_ffn_up[:, inner], w_ffn_down[inner].T]
        return jnp.concatenate(
            [padded_cols(part, wide) for part in parts] + [w_out[outer].T], 1
        )

    def of_heads(array, width):
        shaped = array.reshape(array.shape[0], groups, 2, 2, per_quarter * width)
        mine = jnp.where(side == 0, shaped[:, :, 0], shaped[:, :, 1])
        mine = jnp.where(core == 0, mine[:, :, 0], mine[:, :, 1])
        return mine.reshape(array.shape[0], heads, width)

    mix_parts = gather_weights(mix_half(0), mix_half(1))
    dealt = dealt_by_sequence(tokens)
    dealt, w_ffn_gate, w_ffn_up, w_ffn_down, w_out = lax.optimization_barrier(
        (dealt, w_ffn_gate, w_ffn_up, w_ffn_down, w_out)
    )
    norm_gain, ffn_gain = to_gather_order(norm_gain), to_gather_order(ffn_gain)
    own = to_gather_order(dealt).astype(jnp.float32)
    normed_own = (rms_rows(own) * norm_gain).astype(low)
    normed = with_group(normed_own).reshape(flat, model)
    rest_parts = gather_weights(rest_half(0), rest_half(1))
    w_mix = whole_rows(mix_parts, 0, per_quarter * HEAD)
    pre = matmul(normed, w_mix).reshape(seqs, length, heads * HEAD)
    pre, d_mixed = lax.optimization_barrier((pre, d_mixed))
    rim = jnp.zeros((seqs, RIM, heads * HEAD), jnp.float32)
    if pieces > 1:
        rim = passed_along(pre[:, length - RIM :], "cg", 1)
    starts_own = lax.dynamic_slice_in_dim(seg_starts, lane * own_seqs, own_seqs, 0)
    starts = with_partner(starts_own.astype(jnp.float32)).astype(jnp.int32)
    base = place * length
    seg_ext = seg_ids(starts, base + jnp.arange(-3, length, dtype=jnp.int32))
    segs = jnp.stack(
        [seg_ext[:, 3 - n : 3 - n + length].reshape(seqs, count, CHUNK) for n in range(4)], 2
    ).astype(jnp.float32)
    segs = jnp.pad(segs, ((0, 0), (0, 0), (0, 4), (0, 0)))
    taps = jnp.concatenate(
        [of_heads(conv_query, KEY), of_heads(conv_key, KEY), of_heads(conv_value, VAL)], 2
    ).reshape(4, heads * GATE_AT)
    par = jnp.stack(
        [of_heads(-jnp.exp(a_log)[None], 1)[0, :, 0], of_heads(dt_bias[None], 1)[0, :, 0]], 1
    )
    par = jnp.broadcast_to(
        jnp.pad(par, ((0, 0), (0, 6)))[:, :, None], (heads, 8, 128)
    )
    gain_row = out_gain[None]
    front = (pre, rim, taps, par, segs)
    cot_own = dealt_by_sequence(d_mixed)
    if pieces == 1:
        inverse, step, read, states, mixer, gated = run_whole(*front, gain_row)
    else:
        inverse, step, push, read, base_out, end_map, end_push = run_front(*front)
        state_in = passed_along(end_push, "cg", 1)
        state_in = lax.fori_loop(
            0,
            pieces - 2,
            lambda turn, state: passed_along(apply_map(end_map, state) + end_push, "cg", 1),
            state_in,
        )
        states, mixer, gated = run_output(state_in, step, push, read, base_out, pre, gain_row)
    gated, cot_own = lax.optimization_barrier((gated, cot_own))
    cot_own = to_gather_order(cot_own)
    cot = with_group(cot_own)
    gated_flat = gated.reshape(flat, heads * VAL)
    w_pair = jnp.concatenate(
        [whole_rows(rest_parts, 0, wide), whole_rows(rest_parts, wide, wide)], 1
    )
    w_down_t = whole_rows(rest_parts, 2 * wide, wide)
    w_out_t = whole_rows(rest_parts, 3 * wide, val_cols)
    attn_part = matmul_right_t(gated_flat, w_out_t).astype(low)
    attn_part, cot = lax.optimization_barrier((attn_part, cot))
    cot = cot.reshape(flat, model)
    middle = own + sum_in_group(attn_part.reshape(seqs, length, model))
    normed_two_own = (rms_rows(middle) * ffn_gain).astype(low)
    normed_two = with_group(normed_two_own).reshape(flat, model)
    width = groups * wide
    pair = matmul(normed_two, w_pair)
    gate_pre, up_pre = pair[:, :width], pair[:, width:]
    sigma = jax.nn.sigmoid(gate_pre)
    hidden = (gate_pre * sigma * up_pre).astype(low)
    d_hidden = matmul(cot, w_down_t)
    d_gate_pre = (d_hidden * up_pre * sigma * (1.0 + gate_pre * (1.0 - sigma))).astype(low)
    d_up_pre = (d_hidden * gate_pre * sigma).astype(low)
    d_pair = jnp.concatenate([d_gate_pre, d_up_pre], 1)
    ffn_terms = matmul_right_t(d_pair, w_pair).astype(low)
    d_normed_two = sum_in_group(ffn_terms.reshape(seqs, length, model))
    _, norm_two_back = jax.vjp(norm_scaled, middle, ffn_gain)
    d_middle_part, grad_ffn_gain = norm_two_back(d_normed_two)
    d_middle = cot_own.astype(jnp.float32) + d_middle_part
    grad_pair = matmul_left_t(normed_two, d_pair).astype(low)
    grad_down = matmul_left_t(cot, hidden).astype(low)
    rest_joined = joined_grads(
        zip(
            columns_of(grad_pair[:, :width], groups),
            columns_of(grad_pair[:, width:], groups),
            columns_of(grad_down, groups),
        )
    )
    d_branch = with_group(d_middle.astype(low)).reshape(flat, model)
    ffn_part = matmul_right_t(hidden, w_down_t).astype(low)
    ffn_both = sum_of_cores(ffn_part.reshape(seqs, length, model))
    d_branch, rest_joined, ffn_both = lax.optimization_barrier((d_branch, rest_joined, ffn_both))
    rest_first, rest_second = scatter_grads(rest_joined)
    d_gated = matmul(d_branch, w_out_t).reshape(seqs, length, heads * VAL)
    if pieces == 1:
        ends = (read,)
    else:
        pull, d_start = run_pull(d_gated, mixer, pre, gain_row, step, read)
        d_end = passed_along(d_start, "cg", -1)
        d_end = lax.fori_loop(
            0,
            pieces - 2,
            lambda turn, state: passed_along(apply_map_t(end_map, state) + d_start, "cg", -1),
            d_end,
        )
        ends = (pull, d_end)
    ffn_own = sum_of_sides(ffn_both)
    d_all, d_rim, d_small = run_back(*front, inverse, step, states, d_gated, mixer, gain_row, *ends)
    d_all, ffn_own = lax.optimization_barrier((d_all, ffn_own))
    mixed = dealt_by_tokens(to_model_order((middle + ffn_own).astype(low)))
    if pieces > 1:
        back_rim = passed_along(d_rim, "cg", -1).reshape(seqs, RIM, heads, GATE_AT)
        back_rim = jnp.pad(back_rim, ((0, 0),) * 3 + ((0, HEAD - GATE_AT),))
        tail = d_all[:, length - RIM :].astype(jnp.float32) + back_rim.reshape(seqs, RIM, -1)
        d_all = lax.dynamic_update_slice(d_all, tail.astype(low), (0, length - RIM, 0))
    d_all = d_all.reshape(flat, heads * HEAD)
    grad_mix = matmul_left_t(normed, d_all).astype(low)
    grad_out = matmul_left_t(d_branch, gated_flat).astype(low)
    mix_joined = joined_grads(zip(columns_of(grad_mix, groups), columns_of(grad_out, groups)))
    mix_joined, rest_first, rest_second, d_all = lax.optimization_barrier(
        (mix_joined, rest_first, rest_second, d_all)
    )
    mix_first, mix_second = scatter_grads(mix_joined)
    d_normed = matmul_right_t(d_all, w_mix).astype(low)
    own_d_normed = sum_in_group(d_normed.reshape(seqs, length, model))
    _, norm_back = jax.vjp(norm_scaled, own, norm_gain)
    d_own, grad_norm_gain = norm_back(own_d_normed)
    grad_tokens = dealt_by_tokens(to_model_order((d_middle + d_own).astype(low)))
    grad_tokens = grad_tokens.astype(jnp.float32)
    grad_norm_gain, grad_ffn_gain = to_model_order(grad_norm_gain), to_model_order(grad_ffn_gain)

    small = jnp.sum(d_small, axis=0)

    def placed(part):
        rows, _, each = part.shape
        shaped = part.reshape(rows, groups, 1, 1, per_quarter * each)
        spots = jnp.arange(4).reshape(1, 1, 2, 2, 1)
        return jnp.where(spots == 2 * side + core, shaped, 0.0).reshape(-1)

    conv_parts = jnp.transpose(small[:, :4], (1, 0, 2))
    items = [
        grad_ffn_gain,
        placed(conv_parts[..., :KEY]),
        placed(conv_parts[..., KEY : 2 * KEY]),
        placed(conv_parts[..., 2 * KEY :]),
        jnp.sum(small[:, 4, :VAL], axis=0),
        placed(small[None, :, 5, :1]),
        placed(small[None, :, 6, :1]),
    ]
    sizes = [item.shape[0] for item in items]
    total = up_to(sum(sizes), 1024)
    joined = jnp.concatenate(items + [jnp.zeros((total - sum(sizes),), jnp.float32)])
    joined = summed_everywhere(joined.reshape(-1, 128)).reshape(-1)
    norm_sum = summed_everywhere(grad_norm_gain.reshape(8, -1)).reshape(-1)
    ends = [sum(sizes[: n + 1]) for n in range(len(sizes))]
    sums = [joined[end - size : end] for size, end in zip(sizes, ends)]

    def mix_cols(first, width):
        halves_of = [
            half[:, : per_quarter * HEAD].reshape(half.shape[0], per_quarter, HEAD)[:, :, first : first + width].reshape(
                half.shape[0], -1
            )
            for half in (mix_first, mix_second)
        ]
        return jnp.concatenate(halves_of, 1)

    def rest_cols(first, width, pair=(rest_first, rest_second)):
        return jnp.concatenate([half[:, first : first + width] for half in pair], 1)

    return (
        mixed,
        grad_tokens,
        norm_sum,
        mix_cols(0, KEY),
        mix_cols(KEY, KEY),
        mix_cols(2 * KEY, VAL),
        mix_cols(GATE_AT, VAL),
        mix_cols(AB_AT, 1),
        mix_cols(AB_AT + 1, 1),
        sums[1].reshape(4, -1),
        sums[2].reshape(4, -1),
        sums[3].reshape(4, -1),
        sums[5],
        sums[6],
        sums[4],
        rest_cols(per_quarter * HEAD, val_cols, (mix_first, mix_second)).T,
        sums[0],
        rest_cols(0, half_units),
        rest_cols(wide, half_units),
        rest_cols(2 * wide, half_units).T,
    )


def solution(mesh):
    sizes = tuple(mesh.shape[axis] for axis in ("dp", "ctx", "tensor"))
    fine = Mesh(
        mesh.devices.reshape(sizes[0] // 2, 2, sizes[1] // 2, 2, sizes[2]),
        ("px", "core", "cg", "cl", "tensor"),
    )
    dp = ("px", "core")
    rows = P(("px", "core", "cg", "cl"), "tensor")
    cols = P("tensor", ("px", "core", "cg", "cl"))
    own = P(dp, ("cg", "cl", "tensor"), None)
    return jax.shard_map(
        shards,
        mesh=fine,
        in_specs=(own, P(dp, None), P())
        + (rows,) * 6
        + (P(),) * 6
        + (cols, P(), rows, rows, cols, own),
        out_specs=(own, own, P())
        + (rows,) * 6
        + (P(),) * 6
        + (cols, P(), rows, rows, cols),
        check_vma=False,
    )
```

```python
from functools import partial

import jax
import jax.numpy as jnp
from jax import lax
from jax.experimental import pallas as pl
from jax.experimental.pallas import tpu as pltpu
from jax.sharding import Mesh, PartitionSpec as P

CHUNK = 128
RIM = 8
EPS_NORM = 1e-05
EPS_UNIT = 1e-06
FULL_ACCURACY = lax.Precision.HIGHEST
NN = (((1,), (0,)), ((), ()))
NT = (((1,), (1,)), ((), ()))
TN = (((0,), (0,)), ((), ()))


def dot_low(left, right, dims):
    return lax.dot_general(
        left.astype(jnp.bfloat16),
        right.astype(jnp.bfloat16),
        dims,
        preferred_element_type=jnp.float32,
    )


def halves(value):
    high = value.astype(jnp.bfloat16)
    return high, (value - high.astype(jnp.float32)).astype(jnp.bfloat16)


def dot_split(left, right, dims):
    left_high, left_low = halves(left)
    right_high, right_low = halves(right)
    total = lax.dot_general(left_high, right_high, dims, preferred_element_type=jnp.float32)
    total += lax.dot_general(left_high, right_low, dims, preferred_element_type=jnp.float32)
    return total + lax.dot_general(left_low, right_high, dims, preferred_element_type=jnp.float32)


def sigmoid(value):
    return 1.0 / (1.0 + jnp.exp(-value))


def positions():
    row = lax.broadcasted_iota(jnp.int32, (CHUNK, CHUNK), 0)
    col = lax.broadcasted_iota(jnp.int32, (CHUNK, CHUNK), 1)
    return row, col


def dot_wide(left, right):
    left_high, left_low = halves(left)
    right_high, right_low = halves(right)
    lefts = jnp.concatenate([left_high, left_low], axis=1)
    rights = jnp.concatenate(
        [
            jnp.concatenate([right_high, right_low], axis=1),
            jnp.concatenate([right_high, jnp.zeros_like(right_low)], axis=1),
        ],
        axis=0,
    )
    both = lax.dot_general(lefts, rights, NN, preferred_element_type=jnp.float32)
    return both[:, :CHUNK] + both[:, CHUNK:]


def unit_lower_inverses(lowers):
    row, col = positions()
    eye = (row == col).astype(jnp.float32)
    diag = [jnp.where(row // 8 == col // 8, low, 0.0) for low in lowers]
    result = [eye - d for d in diag]
    power = [dot_wide(d, d) for d in diag]
    result = [x + dot_wide(x, p) for x, p in zip(result, power)]
    power = [dot_wide(p, p) for p in power]
    result = [x + dot_wide(x, p) for x, p in zip(result, power)]
    size = 8
    while size < CHUNK:
        across = (row // (2 * size) == col // (2 * size)) & (row // size != col // size)
        mixed = [dot_wide(jnp.where(across, low, 0.0), x) for low, x in zip(lowers, result)]
        result = [x - dot_wide(x, m) for x, m in zip(result, mixed)]
        size *= 2
    return result


KEY = 128
VAL = 256
GATE_AT = 2 * KEY + VAL
AB_AT = GATE_AT + VAL
HEAD = AB_AT + 128
VMEM_BYTES = 48 * 2**20


def thirds(value):
    high = value.astype(jnp.bfloat16)
    rest = value - high.astype(jnp.float32)
    middle = rest.astype(jnp.bfloat16)
    return high, middle, (rest - middle.astype(jnp.float32)).astype(jnp.bfloat16)


def dot_ones(ones, value, dims):
    left = ones.astype(jnp.bfloat16)
    return sum(
        lax.dot_general(left, part, dims, preferred_element_type=jnp.float32)
        for part in thirds(value)
    )


def unit(values):
    scale = lax.rsqrt(jnp.sum(values * values, axis=-1, keepdims=True) + EPS_UNIT)
    return values * scale, scale


def last_value(column):
    return column[CHUNK - 1 : CHUNK, :]


def spread_lanes(column):
    return jnp.broadcast_to(column, (CHUNK, CHUNK))


def chunk_parts(pre, par, segs, index):
    rows = slice(index * CHUNK, (index + 1) * CHUNK)
    row, col = positions()
    tile = segs[0, index]
    columns = jnp.concatenate([tile, jnp.zeros((CHUNK - 8, CHUNK), jnp.float32)], axis=0).T
    seg = columns[:, 0:1]
    masks = [(seg == columns[:, n : n + 1]).astype(jnp.float32) for n in range(1, 4)]
    shifted = pre[0, rows, AB_AT : AB_AT + 1] + par[0, 1:2, 0:1]
    strength = sigmoid(pre[0, rows, AB_AT + 1 : AB_AT + 2])
    soft = jnp.maximum(shifted, 0.0) + jnp.log1p(jnp.exp(-jnp.abs(shifted)))
    decay = par[0, 0:1, 0:1] * soft
    lower = (row >= col).astype(jnp.float32)
    cumul = dot_ones(lower, spread_lanes(decay), NN)
    allowed = (row >= col) & (seg == tile[0:1, :])
    within = jnp.where(allowed, jnp.exp(jnp.minimum(cumul - cumul.T, 0.0)), 0.0)
    cum = cumul[:, 0:1]
    opening = jnp.where(seg == tile[1:2, 0:1], jnp.exp(cum), 0.0)
    closing = jnp.where(
        seg == tile[0:1, CHUNK - 1 :], jnp.exp(jnp.minimum(last_value(cum) - cum, 0.0)), 0.0
    )
    return dict(
        rows=rows,
        masks=masks,
        shifted=shifted,
        decay=decay,
        strength=strength,
        opening=opening,
        closing=closing,
        within=within,
    )


def fill_ext(ext, rim, pre):
    ext[0:RIM, :] = rim[0, :, :GATE_AT]
    ext[RIM:, :] = pre[0, :, :GATE_AT]


def conv_chunk(ext, taps, part):
    first = RIM + part["rows"].start
    total = taps[0:1, :] * ext[first : first + CHUNK, :]
    for offset in range(1, 4):
        shifted = ext[first - offset : first - offset + CHUNK, :]
        total = total + taps[offset : offset + 1, :] * shifted * part["masks"][offset - 1]
    return total


def split_qkv(array):
    return array[:, :KEY], array[:, KEY : 2 * KEY], array[:, 2 * KEY :]

GROUP = 4


def front_terms(pre, ext, taps, par, segs, first, last):
    row, col = positions()
    eye = (row == col).astype(jnp.float32)
    parts = [chunk_parts(pre, par, segs, n) for n in range(first, last)]
    convs = [conv_chunk(ext, taps, p) for p in parts]
    acts = [split_qkv(c * sigmoid(c)) for c in convs]
    queries = [unit(a[0])[0] * (float(KEY) ** -0.5) for a in acts]
    keys = [unit(a[1])[0] for a in acts]
    inner = [dot_split(k, k, NT) for k in keys]
    lowers = [
        jnp.where(row > col, p["strength"] * p["within"] * i, 0.0) for p, i in zip(parts, inner)
    ]
    inverses = unit_lower_inverses(lowers)
    scores = [dot_low(q, k, NT) * p["within"] for q, k, p in zip(queries, keys, parts)]
    known = [
        dot_low(t, p["strength"] * a[2], NN) for t, p, a in zip(inverses, parts, acts)
    ]
    write = [
        dot_low(t, p["strength"] * p["opening"] * k, NN)
        for t, p, k in zip(inverses, parts, keys)
    ]
    closed = [p["closing"] * k for p, k in zip(parts, keys)]
    steps = [
        last_value(p["opening"]) * eye - dot_low(c, w, TN)
        for p, c, w in zip(parts, closed, write)
    ]
    pushes = [dot_low(c, u, TN) for c, u in zip(closed, known)]
    reads = [
        p["opening"] * q - dot_low(s, w, NN)
        for p, q, s, w in zip(parts, queries, scores, write)
    ]
    bases = [dot_low(s, u, NN) for s, u in zip(scores, known)]
    return inverses, steps, pushes, reads, bases


def write_output(state, base, read, pre, gain, rows, mixer_out, gated_out):
    mixer = base + dot_low(read, state, NN)
    mixer_out[0, 0, rows, :] = mixer
    scale = lax.rsqrt(jnp.mean(mixer * mixer, axis=-1, keepdims=True) + EPS_NORM)
    gate = pre[0, rows, GATE_AT:AB_AT]
    gated_out[0, rows, :] = (mixer * scale * gain[...] * gate * sigmoid(gate)).astype(
        jnp.bfloat16
    )


def chunk_rows(number):
    return slice(number * CHUNK, (number + 1) * CHUNK)


def front_kernel(
    pre, rim, taps, par, segs,
    inverse_out, step_out, push_out, read_out, base_out, end_map, end_push,
    ext,
):
    count = pre.shape[1] // CHUNK
    fill_ext(ext, rim, pre)
    total_map = total_push = None
    for first in range(0, count, GROUP):
        last = min(count, first + GROUP)
        terms = front_terms(pre, ext, taps, par, segs, first, last)
        for n in range(first, last):
            rows = chunk_rows(n)
            inverse, step, push, read, base = (term[n - first] for term in terms)
            inverse_out[0, 0, rows, :] = inverse
            step_out[0, 0, rows, :] = step
            push_out[0, 0, rows, :] = push
            read_out[0, 0, rows, :] = read
            base_out[0, 0, rows, :] = base
            if n:
                total_push = dot_low(step, total_push, NN) + push
                total_map = dot_low(step, total_map, NN)
            else:
                total_map, total_push = step, push
    end_map[0, 0] = total_map
    end_push[0, 0] = total_push


def whole_kernel(
    pre, rim, taps, par, segs, gain,
    inverse_out, step_out, read_out, states_out, mixer_out, gated_out,
    ext,
):
    count = pre.shape[1] // CHUNK
    fill_ext(ext, rim, pre)
    state = jnp.zeros((KEY, VAL), jnp.float32)
    for first in range(0, count, GROUP):
        last = min(count, first + GROUP)
        terms = front_terms(pre, ext, taps, par, segs, first, last)
        for n in range(first, last):
            rows = chunk_rows(n)
            inverse, step, push, read, base = (term[n - first] for term in terms)
            inverse_out[0, 0, rows, :] = inverse
            step_out[0, 0, rows, :] = step
            read_out[0, 0, rows, :] = read
            states_out[0, 0, rows, :] = state
            write_output(state, base, read, pre, gain, rows, mixer_out, gated_out)
            state = dot_low(step, state, NN) + push


def output_kernel(
    state_in, step, push, read, base, pre, gain, states_out, mixer_out, gated_out
):
    count = step.shape[2] // CHUNK
    state = state_in[0, 0]
    for n in range(count):
        rows = chunk_rows(n)
        states_out[0, 0, rows, :] = state
        write_output(
            state, base[0, 0, rows, :], read[0, 0, rows, :], pre, gain, rows, mixer_out, gated_out
        )
        if n < count - 1:
            state = dot_low(step[0, 0, rows, :], state, NN) + push[0, 0, rows, :]


def mixer_back(d_gated, mixer_in, pre, gain, rows):
    mixer = mixer_in[0, 0, rows, :]
    scale = lax.rsqrt(jnp.mean(mixer * mixer, axis=-1, keepdims=True) + EPS_NORM)
    normed = mixer * scale
    gate = pre[0, rows, GATE_AT:AB_AT]
    sig = sigmoid(gate)
    grad = d_gated[0, rows, :]
    through = grad * gate * sig
    d_normed = through * gain[...]
    d_mixer = scale * (d_normed - normed * jnp.mean(d_normed * normed, axis=-1, keepdims=True))
    d_gate = grad * normed * gain[...] * sig * (1.0 + gate * (1.0 - sig))
    return d_mixer, d_gate, jnp.sum(through * normed, axis=0, keepdims=True)


def pull_kernel(d_gated, mixer_in, pre, gain, step, read, pull_out, start_out):
    count = step.shape[2] // CHUNK
    carried = None
    for n in reversed(range(count)):
        rows = slice(n * CHUNK, (n + 1) * CHUNK)
        d_mixer = mixer_back(d_gated, mixer_in, pre, gain, rows)[0]
        pull = dot_low(read[0, 0, rows, :], d_mixer, TN)
        pull_out[0, 0, rows, :] = pull
        if carried is None:
            carried = pull
        else:
            carried = dot_low(step[0, 0, rows, :], carried, TN) + pull
    start_out[0, 0] = carried


def back_kernel(alone, pre, rim, taps, par, segs, inverse, step, states, d_gated, mixer_in, gain, *refs):
    if alone:
        read, d_all_out, d_rim_out, d_small_out, ext, pad = refs
    else:
        pull, d_end, d_all_out, d_rim_out, d_small_out, ext, pad = refs
    length = pre.shape[1]
    count = length // CHUNK
    fill_ext(ext, rim, pre)
    row, col = positions()
    lane = col
    last_row = lax.broadcasted_iota(jnp.int32, (CHUNK, 1), 0) == CHUNK - 1
    lower = (row >= col).astype(jnp.float32)
    d_states = [None] * count
    d_states[count - 1] = jnp.zeros((KEY, VAL), jnp.float32) if alone else d_end[0, 0]
    for n in reversed(range(1, count)):
        block = chunk_rows(n)
        if alone:
            d_mixer = mixer_back(d_gated, mixer_in, pre, gain, block)[0]
            back = dot_low(read[0, 0, block, :], d_mixer, TN)
        else:
            back = pull[0, 0, block, :]
        d_states[n - 1] = dot_low(step[0, 0, block, :], d_states[n], TN) + back
    pad[:, 0:RIM, :] = jnp.zeros((4, RIM, GATE_AT), jnp.float32)
    pad[:, RIM + length :, :] = jnp.zeros((4, RIM, GATE_AT), jnp.float32)
    d_gain = jnp.zeros((1, VAL), jnp.float32)
    d_log = jnp.zeros((1, 1), jnp.float32)
    d_bias = jnp.zeros((1, 1), jnp.float32)
    d_taps = [jnp.zeros((1, GATE_AT), jnp.float32) for _ in range(4)]
    for n in range(count):
        part = chunk_parts(pre, par, segs, n)
        block, within = part["rows"], part["within"]
        strength, opening, closing = part["strength"], part["opening"], part["closing"]
        conv = conv_chunk(ext, taps, part)
        sig = sigmoid(conv)
        act_q, act_k, value = split_qkv(conv * sig)
        unit_q, scale_q = unit(act_q)
        key, scale_k = unit(act_k)
        query = unit_q * (float(KEY) ** -0.5)
        state, d_state = states[0, 0, block, :], d_states[n]
        solve = inverse[0, 0, block, :]
        grad, d_gate, d_gain_part = mixer_back(d_gated, mixer_in, pre, gain, block)
        d_gain = d_gain + d_gain_part
        rest = value - opening * dot_low(key, state, NN)
        update = dot_low(solve, strength * rest, NN)
        scores = dot_low(query, key, NT) * within
        inner = dot_low(key, key, NT) * within
        closed = closing * key
        d_update = dot_low(scores, grad, TN) + dot_low(closed, d_state, NN)
        d_right = dot_low(solve, d_update, TN)
        d_scores = dot_low(grad, update, NT)
        d_lower = jnp.where(row > col, -dot_low(d_right, update, NT), 0.0)
        d_plain = d_scores * within
        d_inner = d_lower * strength * within
        read_back = dot_low(grad, state, NT)
        known_back = -dot_low(strength * d_right, state, NT)
        closed_back = dot_low(update, d_state, NT)
        d_query = opening * read_back + dot_low(d_plain, key, NN)
        d_key = (
            dot_low(d_plain, query, TN)
            + dot_low(d_inner, key, NN)
            + dot_low(d_inner, key, TN)
            + opening * known_back
            + closing * closed_back
        )
        lower_parts = d_lower * inner
        d_strength = jnp.sum(lower_parts, axis=1, keepdims=True) + jnp.sum(
            d_right * rest, axis=1, keepdims=True
        )
        spread = d_scores * scores + strength * lower_parts
        d_opening = jnp.sum(query * read_back + key * known_back, axis=1, keepdims=True)
        d_closing = jnp.sum(key * closed_back, axis=1, keepdims=True) * closing
        through = jnp.sum(
            jnp.sum(state * d_state, axis=1, keepdims=True), axis=0, keepdims=True
        )
        end_sum = jnp.sum(d_closing, axis=0, keepdims=True) + through * last_value(opening)
        d_cumul = (
            jnp.sum(spread, axis=1, keepdims=True)
            + d_opening * opening
            - d_closing
            + jnp.where(last_row, end_sum, 0.0)
        )
        down = spread_lanes(jnp.sum(spread, axis=0, keepdims=True)).T
        d_decay = dot_ones(lower, spread_lanes(d_cumul) - down, TN)[:, 0:1]
        d_alpha = d_decay * par[0, 0:1, 0:1] * sigmoid(part["shifted"])
        d_beta = d_strength * strength * (1.0 - strength)
        d_log = d_log + jnp.sum(d_decay * part["decay"], axis=0, keepdims=True)
        d_bias = d_bias + jnp.sum(d_alpha, axis=0, keepdims=True)
        d_all_out[0, block, GATE_AT:AB_AT] = d_gate.astype(jnp.bfloat16)
        d_all_out[0, block, AB_AT:] = jnp.where(
            lane == 0, d_alpha, jnp.where(lane == 1, d_beta, 0.0)
        ).astype(jnp.bfloat16)
        d_query = d_query * (float(KEY) ** -0.5)
        d_act = jnp.concatenate(
            [
                scale_q * (d_query - unit_q * jnp.sum(unit_q * d_query, axis=-1, keepdims=True)),
                scale_k * (d_key - key * jnp.sum(key * d_key, axis=-1, keepdims=True)),
                strength * d_right,
            ],
            axis=1,
        )
        d_conv = d_act * sig * (1.0 + conv * (1.0 - sig))
        first = RIM + block.start
        for offset in range(4):
            masked = d_conv if offset == 0 else d_conv * part["masks"][offset - 1]
            shifted = ext[first - offset : first - offset + CHUNK, :]
            d_taps[offset] = d_taps[offset] + jnp.sum(masked * shifted, axis=0, keepdims=True)
            pad[offset, first : first + CHUNK, :] = masked * taps[offset : offset + 1, :]
    d_rim = pad[0, 0:RIM, :]
    for offset in range(1, 4):
        d_rim = d_rim + pad[offset, offset : offset + RIM, :]
    d_rim_out[0] = d_rim
    for n in range(count):
        first = RIM + n * CHUNK
        total = pad[0, first : first + CHUNK, :]
        for offset in range(1, 4):
            total = total + pad[offset, first + offset : first + offset + CHUNK, :]
        d_all_out[0, n * CHUNK : (n + 1) * CHUNK, :GATE_AT] = total.astype(jnp.bfloat16)
    for offset in range(4):
        d_small_out[0, 0, offset : offset + 1, :] = d_taps[offset]
    d_small_out[0, 0, 4:5, :] = jnp.concatenate([d_gain, d_gain], axis=1)
    d_small_out[0, 0, 5:6, :] = jnp.broadcast_to(d_log, (1, GATE_AT))
    d_small_out[0, 0, 6:7, :] = jnp.broadcast_to(d_bias, (1, GATE_AT))
    d_small_out[0, 0, 7:8, :] = jnp.zeros((1, GATE_AT), jnp.float32)


def per_head(*tail):
    return pl.BlockSpec((1, 1) + tail, lambda s, h: (s, h) + (0,) * len(tail))


def lanes_at(rows, width):
    return pl.BlockSpec((1, rows, width), lambda s, h: (s, 0, h))


def front_specs(length):
    return [
        lanes_at(length, HEAD),
        lanes_at(RIM, HEAD),
        pl.BlockSpec((4, GATE_AT), lambda s, h: (0, h)),
        pl.BlockSpec((1, 8, 128), lambda s, h: (h, 0, 0)),
        pl.BlockSpec((1, length // CHUNK, 8, CHUNK), lambda s, h: (s, 0, 0, 0)),
    ]


def gain_spec():
    return pl.BlockSpec((1, VAL), lambda s, h: (0, 0))


def shape(dims, kind=jnp.float32):
    return jax.ShapeDtypeStruct(dims, kind)


def call(kernel, lead, in_specs, outs, scratch, units, args):
    length = args[0].shape[1] if args[0].ndim == 3 else args[1].shape[2]
    flops = lead[0] * lead[1] * length * 128 * 128 * 2 * units
    return pl.pallas_call(
        kernel,
        grid=lead,
        in_specs=in_specs,
        out_specs=[spec for spec, _ in outs],
        out_shape=[kind for _, kind in outs],
        scratch_shapes=[pltpu.VMEM(dims, jnp.float32) for dims in scratch],
        compiler_params=pltpu.CompilerParams(vmem_limit_bytes=VMEM_BYTES),
        cost_estimate=pl.CostEstimate(
            flops=flops, bytes_accessed=flops // 100, transcendentals=0
        ),
    )(*args)


def run_front(pre, rim, taps, par, segs):
    seqs, length, wide = pre.shape
    lead = (seqs, wide // HEAD)
    widths = (KEY, KEY, VAL, KEY, VAL)
    outs = [(per_head(length, width), shape(lead + (length, width))) for width in widths]
    outs += [(per_head(KEY, width), shape(lead + (KEY, width))) for width in (KEY, VAL)]
    return call(
        front_kernel,
        lead,
        front_specs(length),
        outs,
        [(length + RIM, GATE_AT)],
        60,
        (pre, rim, taps, par, segs),
    )


def run_output(state_in, step, push, read, base, pre, gain):
    seqs, heads, length, _ = step.shape
    lead = (seqs, heads)
    in_specs = [per_head(KEY, VAL)]
    in_specs += [per_head(length, width) for width in (KEY, VAL, KEY, VAL)]
    in_specs += [lanes_at(length, HEAD), gain_spec()]
    outs = [
        (per_head(length, VAL), shape(lead + (length, VAL))),
        (per_head(length, VAL), shape(lead + (length, VAL))),
        (lanes_at(length, VAL), shape((seqs, length, heads * VAL), jnp.bfloat16)),
    ]
    args = (state_in, step, push, read, base, pre, gain)
    return call(output_kernel, lead, in_specs, outs, [], 15, args)


def run_pull(d_gated, mixer, pre, gain, step, read):
    seqs, heads, length, _ = step.shape
    lead = (seqs, heads)
    in_specs = [lanes_at(length, VAL), per_head(length, VAL), lanes_at(length, HEAD)]
    in_specs += [gain_spec(), per_head(length, KEY), per_head(length, KEY)]
    outs = [
        (per_head(length, VAL), shape(lead + (length, VAL))),
        (per_head(KEY, VAL), shape(lead + (KEY, VAL))),
    ]
    return call(
        pull_kernel, lead, in_specs, outs, [], 15, (d_gated, mixer, pre, gain, step, read)
    )


def run_whole(pre, rim, taps, par, segs, gain):
    seqs, length, wide = pre.shape
    heads = wide // HEAD
    lead = (seqs, heads)
    widths = (KEY, KEY, KEY, VAL, VAL)
    outs = [(per_head(length, width), shape(lead + (length, width))) for width in widths]
    outs.append((lanes_at(length, VAL), shape((seqs, length, heads * VAL), jnp.bfloat16)))
    return call(
        whole_kernel,
        lead,
        front_specs(length) + [gain_spec()],
        outs,
        [(length + RIM, GATE_AT)],
        70,
        (pre, rim, taps, par, segs, gain),
    )


def run_back(pre, rim, taps, par, segs, inverse, step, states, d_gated, mixer, gain, *ends):
    seqs, length, wide = pre.shape
    heads = wide // HEAD
    lead = (seqs, heads)
    alone = len(ends) == 1
    in_specs = front_specs(length)
    in_specs += [per_head(length, width) for width in (KEY, KEY, VAL)]
    in_specs += [lanes_at(length, VAL), per_head(length, VAL), gain_spec()]
    in_specs += [per_head(length, KEY)] if alone else [per_head(length, VAL), per_head(KEY, VAL)]
    outs = [
        (lanes_at(length, HEAD), shape((seqs, length, wide), jnp.bfloat16)),
        (lanes_at(RIM, GATE_AT), shape((seqs, RIM, heads * GATE_AT))),
        (per_head(8, GATE_AT), shape(lead + (8, GATE_AT))),
    ]
    scratch = [(length + RIM, GATE_AT), (4, length + 2 * RIM, GATE_AT)]
    args = (pre, rim, taps, par, segs, inverse, step, states)
    args += (d_gated, mixer, gain) + ends
    return call(partial(back_kernel, alone), lead, in_specs, outs, scratch, 60, args)


def passed_along(value, axis, steps):
    count = lax.axis_size(axis)
    first, last = (max(0, -steps), min(count, count - steps))
    return lax.ppermute(value, axis, [(source, source + steps) for source in range(first, last)])


def swapped(value, axis, bits):
    count = lax.axis_size(axis)
    return lax.ppermute(value, axis, [(place, place ^ bits) for place in range(count)])


def summed_everywhere(value):
    for axis in ("core", "px", "cg", "cl", "tensor"):
        bits = 1
        while bits < lax.axis_size(axis):
            value = value + swapped(value, axis, bits)
            bits *= 2
    return value


def seg_ids(starts, spots):
    return jnp.sum((starts[:, None, :] <= spots[None, :, None]).astype(jnp.int32), axis=2) - 1


def rms_rows(values):
    return values * lax.rsqrt(jnp.mean(values * values, axis=-1, keepdims=True) + EPS_NORM)


def norm_scaled(values, gain):
    return rms_rows(values) * gain


def matmul(left, right):
    return lax.dot_general(left, right, NN, preferred_element_type=jnp.float32)


def matmul_left_t(left, right):
    return lax.dot_general(left, right, TN, preferred_element_type=jnp.float32)


def matmul_right_t(left, right):
    return lax.dot_general(left, right, NT, preferred_element_type=jnp.float32)


def apply_map(linear, state):
    return jnp.einsum("shij,shjv->shiv", linear, state, precision=FULL_ACCURACY)


def apply_map_t(linear, state):
    return jnp.einsum("shji,shjv->shiv", linear, state, precision=FULL_ACCURACY)


def dealt_by_sequence(own):
    lane, lanes = lax.axis_index("tensor"), lax.axis_size("tensor")
    each = own.shape[0] // lanes
    tokens = own.shape[1]
    result = jnp.zeros((each, tokens * lanes) + own.shape[2:], own.dtype)
    for bits in range(lanes):
        other = lane ^ bits
        part = lax.dynamic_slice_in_dim(own, other * each, each, 0)
        if bits:
            part = swapped(part, "tensor", bits)
        result = lax.dynamic_update_slice_in_dim(result, part, other * tokens, 1)
    return result


def dealt_by_tokens(rows):
    lane, lanes = lax.axis_index("tensor"), lax.axis_size("tensor")
    each, tokens = rows.shape[0], rows.shape[1] // lanes
    result = jnp.zeros((each * lanes, tokens) + rows.shape[2:], rows.dtype)
    for bits in range(lanes):
        other = lane ^ bits
        part = lax.dynamic_slice_in_dim(rows, other * tokens, tokens, 1)
        if bits:
            part = swapped(part, "tensor", bits)
        result = lax.dynamic_update_slice_in_dim(result, part, other * each, 0)
    return result


def with_partner(own):
    return jnp.concatenate([own, swapped(own, "core", 1)], 0)


def with_sides(own):
    side = lax.axis_index("cl")
    tokens = own.shape[1]
    both = jnp.zeros((own.shape[0], 2 * tokens) + own.shape[2:], own.dtype)
    both = lax.dynamic_update_slice_in_dim(both, own, side * tokens, 1)
    both = lax.dynamic_update_slice_in_dim(
        both, swapped(own, "cl", 1), (1 - side) * tokens, 1
    )
    return both


def with_group(own):
    return with_partner(with_sides(own))


def sum_of_cores(partial_sums):
    half = partial_sums.shape[0] // 2
    received = swapped(partial_sums[half:], "core", 1)
    both = partial_sums[:half].astype(jnp.float32) + received.astype(jnp.float32)
    return both.astype(partial_sums.dtype)


def sum_of_sides(both):
    side = lax.axis_index("cl")
    tokens = both.shape[1] // 2
    mine = lax.dynamic_slice_in_dim(both, side * tokens, tokens, 1)
    other = lax.dynamic_slice_in_dim(both, (1 - side) * tokens, tokens, 1)
    return mine.astype(jnp.float32) + swapped(other, "cl", 1).astype(jnp.float32)


def sum_in_group(partial_sums):
    return sum_of_sides(sum_of_cores(partial_sums))


SPREAD = ("tensor", "px", "cg")


def traded(value):
    lanes = lax.axis_size("tensor")
    pairs = [
        (side * lanes + lane, (1 - side) * lanes + (lane ^ 1))
        for side in range(2)
        for lane in range(lanes)
        if lane % 2 != side
    ]
    received = lax.ppermute(value, ("cl", "tensor"), pairs)
    stays = lax.axis_index("cl") == lax.axis_index("tensor") % 2
    return jnp.where(stays, value, received)


def rank_weights(first, second):
    core = lax.axis_index("core")
    mine = jnp.where(core == 0, first, second)
    received = swapped(jnp.where(core == 0, second, first), "core", 1)
    pair = jnp.stack(
        [jnp.where(core == 0, mine, received), jnp.where(core == 0, received, mine)]
    )
    return traded(pair.reshape(-1, mine.shape[1]))


def gather_weights(pair):
    full = lax.all_gather(pair, SPREAD, axis=0, tiled=True)
    return full.reshape(lax.axis_size("tensor") // 2, -1, pair.shape[1])


def whole_rows(gathered, first, width):
    return jnp.concatenate([part[:, first : first + width] for part in gathered], 1)


def block_order():
    px, groups = lax.axis_size("px"), lax.axis_size("cg")
    return [
        ((place * 2 + core) * groups + group) * 2 + side
        for side in range(2)
        for place in range(px)
        for group in range(groups)
        for core in range(2)
    ]


def reordered(array, order):
    width = array.shape[-1] // len(order)
    return jnp.concatenate([array[..., n * width : (n + 1) * width] for n in order], -1)


def to_gather_order(array):
    return reordered(array, block_order())


def to_model_order(array):
    order = block_order()
    return reordered(array, [order.index(n) for n in range(len(order))])


def joined_grads(by_k):
    by_k = [list(parts) for parts in by_k]
    rows = by_k[0][0].shape[0]
    widths = [part.shape[1] for part in by_k[0]]
    joined = jnp.zeros((rows * len(by_k), sum(widths)), by_k[0][0].dtype)
    for n, parts in enumerate(by_k):
        for place, part in enumerate(parts):
            joined = lax.dynamic_update_slice(joined, part, (n * rows, sum(widths[:place])))
    return joined


def scatter_grads(joined):
    return lax.psum_scatter(joined, SPREAD, scatter_dimension=0, tiled=True)


def own_rows_of(summed):
    core = lax.axis_index("core")
    summed = traded(summed)
    rows = summed.shape[0] // 2
    top, bottom = summed[:rows], summed[rows:]
    mine = jnp.where(core == 0, top, bottom)
    received = swapped(jnp.where(core == 0, bottom, top), "core", 1)
    first = jnp.where(core == 0, mine, received).astype(jnp.float32)
    second = jnp.where(core == 0, received, mine).astype(jnp.float32)
    return first, second


def columns_of(array, groups):
    width = array.shape[1] // groups
    return [array[:, n * width : (n + 1) * width] for n in range(groups)]


def padded_cols(array, width):
    return jnp.pad(array, ((0, 0), (0, width - array.shape[1])))


def up_to(value, step):
    return -(-value // step) * step


def shards(
    tokens,
    seg_starts,
    norm_gain,
    w_query,
    w_key,
    w_value,
    w_gate,
    w_alpha,
    w_beta,
    conv_query,
    conv_key,
    conv_value,
    a_log,
    dt_bias,
    out_gain,
    w_out,
    ffn_gain,
    w_ffn_gate,
    w_ffn_up,
    w_ffn_down,
    d_mixed,
):
    low = jnp.bfloat16
    core = lax.axis_index("core")
    lane = lax.axis_index("tensor")
    side = lax.axis_index("cl")
    place = lax.axis_index("cg")
    lanes = lax.axis_size("tensor")
    pieces = lax.axis_size("cg")
    groups = lanes // 2
    model = tokens.shape[2]
    length = 2 * tokens.shape[1] * lanes
    own_seqs = tokens.shape[0] // lanes
    seqs = 2 * own_seqs
    flat = seqs * length
    quarter_heads = w_alpha.shape[1]
    per_quarter = quarter_heads // 2
    heads = per_quarter * groups
    units = w_ffn_gate.shape[1]
    half_units = units // 2
    wide = up_to(half_units, 128)
    val_cols = per_quarter * VAL
    count = length // CHUNK

    def head_block(number):
        key = slice(number * KEY, (number + 1) * KEY)
        val = slice(number * VAL, (number + 1) * VAL)
        one = slice(number, number + 1)
        parts = [w_query[:, key], w_key[:, key], w_value[:, val], w_gate[:, val]]
        return padded_cols(
            jnp.concatenate(parts + [w_alpha[:, one], w_beta[:, one]], 1), HEAD
        )

    def mix_half(half):
        numbers = range(half * per_quarter, (half + 1) * per_quarter)
        return jnp.concatenate([head_block(number) for number in numbers], 1)

    def rest_half(half):
        inner = slice(half * half_units, (half + 1) * half_units)
        outer = slice(half * val_cols, (half + 1) * val_cols)
        parts = [w_ffn_gate[:, inner], w_ffn_up[:, inner], w_ffn_down[inner].T]
        return jnp.concatenate(
            [padded_cols(part, wide) for part in parts] + [w_out[outer].T], 1
        )

    def of_heads(array, width):
        shaped = array.reshape(array.shape[0], groups, 2, 2, per_quarter * width)
        mine = jnp.where(side == 0, shaped[:, :, 0], shaped[:, :, 1])
        mine = jnp.where(core == 0, mine[:, :, 0], mine[:, :, 1])
        return mine.reshape(array.shape[0], heads, width)

    mix_pair = rank_weights(mix_half(0), mix_half(1))
    mix_pair, tokens = lax.optimization_barrier((mix_pair, tokens))
    mix_parts = gather_weights(mix_pair)
    dealt = dealt_by_sequence(tokens)
    norm_gain, ffn_gain = to_gather_order(norm_gain), to_gather_order(ffn_gain)
    own = to_gather_order(dealt).astype(jnp.float32)
    normed_own = (rms_rows(own) * norm_gain).astype(low)
    normed_both = with_sides(normed_own)
    mix_parts, normed_both, w_ffn_gate, w_ffn_up, w_ffn_down, w_out = lax.optimization_barrier(
        (mix_parts, normed_both, w_ffn_gate, w_ffn_up, w_ffn_down, w_out)
    )
    rest_pair = rank_weights(rest_half(0), rest_half(1))
    normed = with_partner(normed_both).reshape(flat, model)
    w_mix = whole_rows(mix_parts, 0, per_quarter * HEAD)
    pre = matmul(normed, w_mix).reshape(seqs, length, heads * HEAD)
    pre, d_mixed, rest_pair = lax.optimization_barrier((pre, d_mixed, rest_pair))
    rest_parts = gather_weights(rest_pair)
    rim = jnp.zeros((seqs, RIM, heads * HEAD), jnp.float32)
    if pieces > 1:
        rim = passed_along(pre[:, length - RIM :], "cg", 1)
    starts_own = lax.dynamic_slice_in_dim(seg_starts, lane * own_seqs, own_seqs, 0)
    starts = with_partner(starts_own.astype(jnp.float32)).astype(jnp.int32)
    base = place * length
    seg_ext = seg_ids(starts, base + jnp.arange(-3, length, dtype=jnp.int32))
    segs = jnp.stack(
        [seg_ext[:, 3 - n : 3 - n + length].reshape(seqs, count, CHUNK) for n in range(4)], 2
    ).astype(jnp.float32)
    segs = jnp.pad(segs, ((0, 0), (0, 0), (0, 4), (0, 0)))
    taps = jnp.concatenate(
        [of_heads(conv_query, KEY), of_heads(conv_key, KEY), of_heads(conv_value, VAL)], 2
    ).reshape(4, heads * GATE_AT)
    par = jnp.stack(
        [of_heads(-jnp.exp(a_log)[None], 1)[0, :, 0], of_heads(dt_bias[None], 1)[0, :, 0]], 1
    )
    par = jnp.broadcast_to(
        jnp.pad(par, ((0, 0), (0, 6)))[:, :, None], (heads, 8, 128)
    )
    gain_row = out_gain[None]
    front = (pre, rim, taps, par, segs)
    cot_own = dealt_by_sequence(d_mixed)
    if pieces == 1:
        inverse, step, read, states, mixer, gated = run_whole(*front, gain_row)
    else:
        inverse, step, push, read, base_out, end_map, end_push = run_front(*front)
        state_in = passed_along(end_push, "cg", 1)
        state_in = lax.fori_loop(
            0,
            pieces - 2,
            lambda turn, state: passed_along(apply_map(end_map, state) + end_push, "cg", 1),
            state_in,
        )
        states, mixer, gated = run_output(state_in, step, push, read, base_out, pre, gain_row)
    gated, cot_own = lax.optimization_barrier((gated, cot_own))
    cot_own = to_gather_order(cot_own)
    cot = with_group(cot_own)
    gated_flat = gated.reshape(flat, heads * VAL)
    w_pair = jnp.concatenate(
        [whole_rows(rest_parts, 0, wide), whole_rows(rest_parts, wide, wide)], 1
    )
    w_down_t = whole_rows(rest_parts, 2 * wide, wide)
    w_out_t = whole_rows(rest_parts, 3 * wide, val_cols)
    attn_part = matmul_right_t(gated_flat, w_out_t).astype(low)
    attn_part, cot = lax.optimization_barrier((attn_part, cot))
    cot = cot.reshape(flat, model)
    middle = own + sum_in_group(attn_part.reshape(seqs, length, model))
    normed_two_own = (rms_rows(middle) * ffn_gain).astype(low)
    normed_two = with_group(normed_two_own).reshape(flat, model)
    width = groups * wide
    pair = matmul(normed_two, w_pair)
    gate_pre, up_pre = pair[:, :width], pair[:, width:]
    sigma = jax.nn.sigmoid(gate_pre)
    hidden = (gate_pre * sigma * up_pre).astype(low)
    d_hidden = matmul(cot, w_down_t)
    d_gate_pre = (d_hidden * up_pre * sigma * (1.0 + gate_pre * (1.0 - sigma))).astype(low)
    d_up_pre = (d_hidden * gate_pre * sigma).astype(low)
    d_pair = jnp.concatenate([d_gate_pre, d_up_pre], 1)
    ffn_terms = matmul_right_t(d_pair, w_pair).astype(low)
    d_normed_two = sum_in_group(ffn_terms.reshape(seqs, length, model))
    _, norm_two_back = jax.vjp(norm_scaled, middle, ffn_gain)
    d_middle_part, grad_ffn_gain = norm_two_back(d_normed_two)
    d_middle = cot_own.astype(jnp.float32) + d_middle_part
    grad_pair = matmul_left_t(normed_two, d_pair).astype(low)
    grad_down = matmul_left_t(cot, hidden).astype(low)
    rest_joined = joined_grads(
        zip(
            columns_of(grad_pair[:, :width], groups),
            columns_of(grad_pair[:, width:], groups),
            columns_of(grad_down, groups),
        )
    )
    d_branch = with_group(d_middle.astype(low)).reshape(flat, model)
    ffn_part = matmul_right_t(hidden, w_down_t).astype(low)
    ffn_both = sum_of_cores(ffn_part.reshape(seqs, length, model))
    rest_summed = scatter_grads(rest_joined)
    d_branch, ffn_both, _ = lax.optimization_barrier((d_branch, ffn_both, rest_joined))
    d_gated = matmul(d_branch, w_out_t).reshape(seqs, length, heads * VAL)
    if pieces == 1:
        ends = (read,)
    else:
        pull, d_start = run_pull(d_gated, mixer, pre, gain_row, step, read)
        d_end = passed_along(d_start, "cg", -1)
        d_end = lax.fori_loop(
            0,
            pieces - 2,
            lambda turn, state: passed_along(apply_map_t(end_map, state) + d_start, "cg", -1),
            d_end,
        )
        ends = (pull, d_end)
    ffn_own = sum_of_sides(ffn_both)
    d_all, d_rim, d_small = run_back(*front, inverse, step, states, d_gated, mixer, gain_row, *ends)
    d_all, ffn_own = lax.optimization_barrier((d_all, ffn_own))
    mixed = dealt_by_tokens(to_model_order((middle + ffn_own).astype(low)))
    if pieces > 1:
        back_rim = passed_along(d_rim, "cg", -1).reshape(seqs, RIM, heads, GATE_AT)
        back_rim = jnp.pad(back_rim, ((0, 0),) * 3 + ((0, HEAD - GATE_AT),))
        tail = d_all[:, length - RIM :].astype(jnp.float32) + back_rim.reshape(seqs, RIM, -1)
        d_all = lax.dynamic_update_slice(d_all, tail.astype(low), (0, length - RIM, 0))
    d_all = d_all.reshape(flat, heads * HEAD)
    grad_mix = matmul_left_t(normed, d_all).astype(low)
    grad_out = matmul_left_t(d_branch, gated_flat).astype(low)
    grad_heads = [
        part.reshape(model, per_quarter, HEAD) for part in columns_of(grad_mix, groups)
    ]
    mix_joined = joined_grads(
        [part[:, n, :AB_AT] for n in range(per_quarter)] + [out]
        for part, out in zip(grad_heads, columns_of(grad_out, groups))
    )
    grad_ab = jnp.concatenate([part[..., AB_AT : AB_AT + 2] for part in grad_heads], 1)
    mix_joined, rest_summed, d_all = lax.optimization_barrier((mix_joined, rest_summed, d_all))
    rest_first, rest_second = own_rows_of(rest_summed)
    mix_first, mix_second = own_rows_of(scatter_grads(mix_joined))
    d_normed = matmul_right_t(d_all, w_mix).astype(low)
    d_normed = sum_of_cores(d_normed.reshape(seqs, length, model))
    d_normed, mixed = lax.optimization_barrier((d_normed, mixed))
    own_d_normed = sum_of_sides(d_normed)
    _, norm_back = jax.vjp(norm_scaled, own, norm_gain)
    d_own, grad_norm_gain = norm_back(own_d_normed)
    grad_tokens = dealt_by_tokens(to_model_order((d_middle + d_own).astype(low)))
    grad_tokens = grad_tokens.astype(jnp.float32)

    small = jnp.sum(d_small, axis=0)

    def placed(part):
        rows, _, each = part.shape
        shaped = part.reshape(rows, groups, 1, 1, per_quarter * each)
        spots = jnp.arange(4).reshape(1, 1, 2, 2, 1)
        return jnp.where(spots == 2 * side + core, shaped, 0.0).reshape(-1)

    conv_parts = jnp.transpose(small[:, :4], (1, 0, 2))
    items = [
        grad_ffn_gain,
        placed(conv_parts[..., :KEY]),
        placed(conv_parts[..., KEY : 2 * KEY]),
        placed(conv_parts[..., 2 * KEY :]),
        jnp.sum(small[:, 4, :VAL], axis=0),
        placed(small[None, :, 5, :1]),
        placed(small[None, :, 6, :1]),
        placed(jnp.transpose(grad_ab, (2, 0, 1)).reshape(-1, heads, 1).astype(jnp.float32)),
    ]
    sizes = [item.shape[0] for item in items]
    total = up_to(sum(sizes), 1024)
    joined = jnp.concatenate(items + [jnp.zeros((total - sum(sizes),), jnp.float32)])
    joined = summed_everywhere(joined.reshape(-1, 128)).reshape(-1)
    norm_sum = summed_everywhere(grad_norm_gain.reshape(8, -1)).reshape(-1)
    ends = [sum(sizes[: n + 1]) for n in range(len(sizes))]
    sums = [joined[end - size : end] for size, end in zip(sizes, ends)]
    blocks = 4 * lax.axis_size("px") * pieces
    block = ((side * lax.axis_size("px") + lax.axis_index("px")) * pieces + place) * 2 + core
    ab_sums = lax.dynamic_slice(
        sums[7].reshape(2, model, lanes * quarter_heads),
        (0, block * (model // blocks), lane * quarter_heads),
        (2, model // blocks, quarter_heads),
    )

    def mix_cols(first, width):
        halves_of = [
            half[:, : per_quarter * AB_AT].reshape(half.shape[0], per_quarter, AB_AT)[:, :, first : first + width].reshape(
                half.shape[0], -1
            )
            for half in (mix_first, mix_second)
        ]
        return jnp.concatenate(halves_of, 1)

    def rest_cols(first, width, pair=(rest_first, rest_second)):
        return jnp.concatenate([half[:, first : first + width] for half in pair], 1)

    return (
        mixed,
        grad_tokens,
        to_model_order(norm_sum),
        mix_cols(0, KEY),
        mix_cols(KEY, KEY),
        mix_cols(2 * KEY, VAL),
        mix_cols(GATE_AT, VAL),
        ab_sums[0],
        ab_sums[1],
        sums[1].reshape(4, -1),
        sums[2].reshape(4, -1),
        sums[3].reshape(4, -1),
        sums[5],
        sums[6],
        sums[4],
        rest_cols(per_quarter * AB_AT, val_cols, (mix_first, mix_second)).T,
        to_model_order(sums[0]),
        rest_cols(0, half_units),
        rest_cols(wide, half_units),
        rest_cols(2 * wide, half_units).T,
    )


def solution(mesh):
    sizes = tuple(mesh.shape[axis] for axis in ("dp", "ctx", "tensor"))
    fine = Mesh(
        mesh.devices.reshape(sizes[0] // 2, 2, sizes[1] // 2, 2, sizes[2]),
        ("px", "core", "cg", "cl", "tensor"),
    )
    dp = ("px", "core")
    rows = P(("px", "core", "cg", "cl"), "tensor")
    cols = P("tensor", ("px", "core", "cg", "cl"))
    own = P(dp, ("cg", "cl", "tensor"), None)
    return jax.shard_map(
        shards,
        mesh=fine,
        in_specs=(own, P(dp, None), P())
        + (rows,) * 6
        + (P(),) * 6
        + (cols, P(), rows, rows, cols, own),
        out_specs=(own, own, P())
        + (rows,) * 6
        + (P(),) * 6
        + (cols, P(), rows, rows, cols),
        check_vma=False,
    )
```
